32 devices in a mesh: grp: 2 (over x), refl: 16 (over z, y, core).
Axes of the slice: x: 2, y: 2, z: 4, core: 2. Of those that a mesh axis runs over, the one named last changes fastest.
Arguments:
- feed_plane: float32 [4, 2048], P('grp', 'refl'), parts along dimension 0, may hold values from -3 to 3
- feed_height: float32 [4096], P(('grp', 'refl')), parts along dimension 0, may hold values from 20 to 24
- feed_weights: bfloat16 [2048, 256], P('refl', 'grp'), parts along dimension 1, may hold values from -0.125 to 0.125
- point_plane: float32 [4, 4096], P('grp', 'refl'), parts along dimension 0, may hold values from -35 to 35
- point_height: float32 [8192], P(('grp', 'refl')), parts along dimension 0, may hold values from 0 to 4
- patch_factor: float32 [8192], P(('grp', 'refl')), parts along dimension 0, may hold values from 0.3 to 3
- direction_cosines: float32 [2, 2048], P(None, 'refl'), may hold values from -0.3 to 0.3
Outputs:
- pattern: float32 [2048, 256], P('refl', 'grp'), parts along dimension 1
The draws below stay inside these ranges and needn't reach their ends.
There are 2 independent parts, one for each index of `grp`. The reference program is written for one: setup_inputs(seed, part) draws one part's arguments, and reference() takes and returns one part's arrays. A program takes and returns all parts, laid end to end along the dimension named above; an argument that names none is the same for every part. Nothing has to cross between parts.
All inputs are finite; a program needn't handle non-finite values.
Results may differ from the reference program's by a relative error of at most 0.0047.
Values may be sent and summed in bfloat16 or wider, within the bound.
No kernel may reach another device: no remote copies, remote signals or barrier semaphores. Data moves between devices by JAX's collectives and lax.ppermute only.
A program may use at most 64 MiB of HBM per device.

```python
import math
import jax
import jax.numpy as jnp
from jax import lax

B = 64
P_DEV = 256
R_DEV = 128
S = 2048
P_SIZE = 4096
R = 2048


def block_levels(own_key, shape, cuts, low, high):
    gain, own = 1.0, jax.random.fold_in(own_key, 6)
    for axis_at, shards_of in cuts:
        steps = jnp.exp(jax.random.uniform(jax.random.fold_in(own, axis_at), (shards_of,), jnp.float32, low / len(cuts), high / len(cuts)))
        gain = gain * jnp.repeat(steps, shape[axis_at] // shards_of).reshape([-1 if axis == axis_at else 1 for axis in range(len(shape))])
    return gain


def gaussian(stream_key, shape, scale, most, split=(), held_as=jnp.bfloat16):
    level = block_levels(stream_key, shape, split, -0.22, 0.18) if split else 1.0
    result = jax.random.normal(stream_key, shape, jnp.float32) * scale * level
    return jnp.minimum(jnp.maximum(result, -most), most).astype(held_as)


def setup_inputs(seed: int = 0, part: int = 0) -> dict:
    key_of = jax.random.split(jax.random.key(seed), 8)
    part_splits = jax.random.split(jax.random.fold_in(key_of[7], part), 8)
    return {
        "feed_plane": jnp.clip(jax.random.uniform(part_splits[0], (2, S), jnp.float32, -3.0, 3.0) * block_levels(part_splits[0], (2, S), ((1, 16),), -0.4, 0.0), -3.0, 3.0),
        "feed_height": jnp.clip(20.0 + 4.0 * jax.random.uniform(part_splits[1], (S,), jnp.float32) ** block_levels(part_splits[1], (S,), ((0, 16),), -0.2, 0.2), 20.0, 24.0),
        "feed_weights": gaussian(part_splits[2], (S, 2 * B), S ** -0.5, 0.125, ((0, 16),)),
        "point_plane": jnp.clip(jax.random.uniform(part_splits[3], (2, P_SIZE), jnp.float32, -35.0, 35.0) * block_levels(part_splits[3], (2, P_SIZE), ((1, 16),), -0.4, 0.0), -35.0, 35.0),
        "point_height": jnp.clip(4.0 * jax.random.uniform(part_splits[4], (P_SIZE,), jnp.float32) ** block_levels(part_splits[4], (P_SIZE,), ((0, 16),), -0.2, 0.2), 0.0, 4.0),
        "patch_factor": jnp.clip(jnp.exp(math.log(3.0) - 2.3025851 * jax.random.uniform(part_splits[5], (P_SIZE,), jnp.float32) ** block_levels(part_splits[5], (P_SIZE,), ((0, 16),), -0.2, 0.2)), 0.3, 3.0),
        "direction_cosines": jnp.clip(jax.random.uniform(key_of[6], (2, R), jnp.float32, -0.3, 0.3) * block_levels(key_of[6], (2, R), ((1, 16),), -0.4, 0.0), -0.3, 0.3),
    }


TWO_PI = 2.0 * math.pi
RANGE_REF = 20.0

def rotate(columns):
    half = columns.shape[1] // 2
    return jnp.concatenate([-columns[:, half:], columns[:, :half]], axis=1)

def green_tile(point_plane, point_height, feed_plane, feed_height):
    across = point_plane[0][:, None] - feed_plane[0][None, :]
    along = point_plane[1][:, None] - feed_plane[1][None, :]
    height = feed_height[None, :] - point_height[:, None]
    squared = across * across + along * along + height * height
    distance = jnp.sqrt(squared)
    amplitude = RANGE_REF * height / squared
    turning = TWO_PI * distance
    return ((amplitude * jnp.cos(turning)).astype(jnp.bfloat16), (-amplitude * jnp.sin(turning)).astype(jnp.bfloat16))

def incident_rows(point_plane, point_height, feed_plane, feed_height, weights, weights_turned):
    in_phase, quadrature = green_tile(point_plane, point_height, feed_plane, feed_height)
    return jnp.dot(in_phase, weights, preferred_element_type=jnp.float32) + jnp.dot(quadrature, weights_turned, preferred_element_type=jnp.float32)

def far_kernel(cosines, point_plane, point_height):
    normal = jnp.sqrt(1.0 - cosines[0] * cosines[0] - cosines[1] * cosines[1])
    turning = TWO_PI * (cosines[0][:, None] * point_plane[0][None, :] + cosines[1][:, None] * point_plane[1][None, :] + normal[:, None] * point_height[None, :])
    return (jnp.cos(turning).astype(jnp.bfloat16), jnp.sin(turning).astype(jnp.bfloat16))

def radiate_rows(cosines, point_plane, point_height, currents, currents_turned):
    in_phase, quadrature = far_kernel(cosines, point_plane, point_height)
    return jnp.dot(in_phase, currents, preferred_element_type=jnp.float32) + jnp.dot(quadrature, currents_turned, preferred_element_type=jnp.float32)

def reference(feed_plane, feed_height, feed_weights, point_plane, point_height, patch_factor, direction_cosines):
    weights_turned = rotate(feed_weights)
    point_count = point_plane.shape[1]
    blocks = point_count // P_DEV
    plane_blocks = point_plane.reshape(2, blocks, P_DEV).transpose(1, 0, 2)
    height_blocks = point_height.reshape(blocks, P_DEV)
    incident = lax.map(lambda pair: incident_rows(pair[0], pair[1], feed_plane, feed_height, feed_weights, weights_turned), (plane_blocks, height_blocks)).reshape(point_count, 2 * B)
    norm_scale = 1.0 / math.sqrt(point_count)
    currents = (incident * (patch_factor * norm_scale)[:, None]).astype(jnp.bfloat16)
    currents_turned = rotate(currents)
    direction_count = direction_cosines.shape[1]
    dir_blocks = direction_count // R_DEV
    cosine_blocks = direction_cosines.reshape(2, dir_blocks, R_DEV).transpose(1, 0, 2)
    pattern = lax.map(lambda cosines: radiate_rows(cosines, point_plane, point_height, currents, currents_turned), cosine_blocks)
    return pattern.reshape(direction_count, 2 * B)
```

```python
import math

import jax
import jax.numpy as jnp
from jax import lax
from jax.experimental import pallas as pl
from jax.experimental.pallas import tpu as pltpu
from jax.sharding import PartitionSpec as P

RANGE_REF = 20.0
F32, BF16 = jnp.float32, jnp.bfloat16

SIN_HALF = (3.1415902835895886, -5.167407697719414, 2.544020810735872, -0.5594899090940457)
COS_HALF = (0.9999932952798736, -4.933938014977294, 4.041283824377777, -1.222127057577997)

COORDS = 5
PACK_ROWS = 16


def horner(square, terms, scale):
    total = jnp.float32(terms[-1] * scale)
    for term in terms[-2::-1]:
        total = total * square + jnp.float32(term * scale)
    return total


def circle(turns, gain):
    part = turns - jnp.round(turns)
    square = part * part
    root = math.sqrt(2.0 * abs(gain))
    half_sin = part * horner(square, SIN_HALF, root)
    half_cos = horner(square, COS_HALF, 2.0 * gain / root)
    return abs(gain) - half_sin * half_sin, half_sin * half_cos


def turned(columns):
    half = columns.shape[1] // 2
    return jnp.concatenate([-columns[:, half:], columns[:, :half]], axis=1)


def pack_body(weights, feed_plane, feed_height, cosines, message):
    rows = weights.shape[0]
    message[:rows, :] = weights[...]
    lanes = weights.shape[1]
    exact = jnp.concatenate([feed_plane[...], feed_height[...], cosines[...]], axis=0)
    high = exact.astype(BF16)
    rest = exact - high.astype(F32)
    middle = rest.astype(BF16)
    low = (rest - middle.astype(F32)).astype(BF16)
    pad = jnp.zeros((PACK_ROWS - 3 * COORDS, lanes), F32)
    message[rows:, :] = jnp.concatenate(
        [high.astype(F32), middle.astype(F32), low.astype(F32), pad], axis=0
    ).astype(BF16)


def unpack(tail):
    tail = tail.astype(F32)
    return (tail[:COORDS] + tail[COORDS : 2 * COORDS]) + tail[2 * COORDS : 3 * COORDS]


def fill_point_columns(points, columns, base):
    lanes = points.shape[1]
    up = points[...].T
    for at in range(2):
        columns[base + at * lanes : base + (at + 1) * lanes, :] = jnp.concatenate(
            [up[:, 2 * k + at : 2 * k + at + 1] for k in range(4)], axis=1
        )


def green_body(has_base, *refs):
    own_points, far_points, messages = refs[:3]
    base = refs[3] if has_base else None
    outs = refs[4:-6] if has_base else refs[3:-6]
    columns, rows, weights, weights_turned, green_re, green_im = refs[-6:]
    count, height, lanes = messages.shape
    sources = height - PACK_ROWS
    half = 2 * lanes
    fill_point_columns(own_points, columns, 0)
    fill_point_columns(far_points, columns, half)
    for at in range(count):
        where = slice(at * sources, (at + 1) * sources)
        rows[0:COORDS, where] = unpack(messages[at, sources:, :])
        block = messages[at, :sources, :]
        weights[where, :] = block
        weights_turned[where, :] = turned(block)
    tile = 16

    def one(at, carry):
        here = pl.ds(pl.multiple_of(at * tile, tile), tile)
        across = columns[here, 0:1] - rows[0:1, :]
        along = columns[here, 1:2] - rows[1:2, :]
        height = rows[2:3, :] - columns[here, 2:3]
        squared = across * across + along * along + height * height
        inverse = lax.rsqrt(squared)
        cosine, sine = circle(squared * inverse, -RANGE_REF)
        amplitude = height * (inverse * inverse)
        green_re[here, :] = (amplitude * cosine).astype(BF16)
        green_im[here, :] = (amplitude * sine).astype(BF16)
        return carry

    lax.fori_loop(0, green_re.shape[0] // tile, one, 0, unroll=2)
    total = jnp.dot(green_re[...], weights[...], preferred_element_type=F32) + jnp.dot(
        green_im[...], weights_turned[...], preferred_element_type=F32
    )
    if has_base:
        total = total + base[...]
    for out in outs:
        out[...] = total.astype(out.dtype)


def kernel_body(own_points, far_points, tails, kernel_re, kernel_im, columns, rows):
    count, _, lanes = tails.shape
    half = 2 * lanes
    for at in range(count):
        uv = unpack(tails[at])[3:5]
        normal = jnp.sqrt(1.0 - uv[0:1] * uv[0:1] - uv[1:2] * uv[1:2])
        pad = jnp.zeros((5, lanes), F32)
        columns[at * lanes : (at + 1) * lanes, :] = jnp.concatenate([uv, normal, pad], axis=0).T
    for base, points in ((0, own_points), (half, far_points)):
        for k in range(3):
            for at in range(2):
                rows[k : k + 1, base + at * lanes : base + (at + 1) * lanes] = points[
                    2 * k + at : 2 * k + at + 1, :
                ]
    tile = 16

    def one(at, carry):
        here = pl.ds(pl.multiple_of(at * tile, tile), tile)
        turns = (
            columns[here, 0:1] * rows[0:1, :]
            + columns[here, 1:2] * rows[1:2, :]
            + columns[here, 2:3] * rows[2:3, :]
        )
        cosine, sine = circle(turns, 1.0)
        kernel_re[here, :] = cosine.astype(BF16)
        kernel_im[here, :] = sine.astype(BF16)
        return carry

    lax.fori_loop(0, kernel_re.shape[0] // tile, one, 0, unroll=2)


def currents_body(scale, mine, theirs, own_points, far_points, currents, columns):
    half = mine.shape[0] // 2
    fill_point_columns(own_points, columns, 0)
    fill_point_columns(far_points, columns, half)
    for here, there in ((slice(0, half), slice(half, None)), (slice(half, None), slice(0, half))):
        field = mine[here, :] + theirs[there, :].astype(F32)
        currents[here, :] = (field * (columns[here, 3:4] * scale)).astype(BF16)


def radiate_body(kernel_re, kernel_im, currents, out):
    held = currents[...]
    out[...] = (
        jnp.dot(kernel_re[...], held, preferred_element_type=F32)
        + jnp.dot(kernel_im[...], turned(held), preferred_element_type=F32)
    ).astype(out.dtype)


def fold_body(mine, theirs, kept, sent):
    first = kept.shape[0]
    total = mine[...] + theirs[...].astype(F32)
    kept[...] = total[:first]
    sent[...] = total[first:].astype(BF16)


def finish_body(kept, *refs):
    total = kept[...]
    for ref in refs[:-1]:
        total = total + ref[...].astype(F32)
    refs[-1][...] = total


def call(body, outs, scratch=(), flops=0, trans=0):
    return pl.pallas_call(
        body,
        out_shape=[jax.ShapeDtypeStruct(*out) for out in outs],
        scratch_shapes=list(scratch),
        compiler_params=pltpu.CompilerParams(vmem_limit_bytes=32 * 1024 * 1024),
        cost_estimate=pl.CostEstimate(flops=flops, bytes_accessed=1 << 20, transcendentals=trans),
    )


def per_device(
    feed_plane,
    feed_height,
    feed_weights,
    point_plane,
    point_height,
    patch_factor,
    direction_cosines,
):
    size = lax.axis_size("refl")
    line = size // 4
    sources, lanes = feed_weights.shape
    local_points = point_height.shape[0]
    half_points = 2 * local_points
    directions = direction_cosines.shape[1]

    def pairs(step):
        out = []
        for at in range(size):
            row, place = divmod(at, 4)
            far, near = divmod(step, 4)
            to = (row ^ far) if line & (line - 1) == 0 else (row + far) % line
            out.append((at, to * 4 + (place ^ near)))
        return out

    def swap(x, step, back=False):
        links = pairs(step)
        return lax.ppermute(x, "refl", [(b, a) for a, b in links] if back else links)

    message = call(pack_body, [((sources + PACK_ROWS, lanes), BF16)])(
        feed_weights, feed_plane, feed_height[None, :], direction_cosines
    )[0]
    points = jnp.concatenate(
        [
            point_plane.reshape(4, lanes),
            point_height.reshape(2, lanes),
            patch_factor.reshape(2, lanes),
        ],
        axis=0,
    )
    far_points = swap(points, 2)
    near_messages = jnp.stack([message] + [swap(message, 4 * k) for k in range(1, line)])
    side_messages = swap(near_messages, 1)

    part = line * sources
    elements = half_points * part
    scratch = [
        pltpu.VMEM((half_points, 4), F32),
        pltpu.VMEM((8, part), F32),
        pltpu.VMEM((part, lanes), BF16),
        pltpu.VMEM((part, lanes), BF16),
        pltpu.VMEM((half_points, part), BF16),
        pltpu.VMEM((half_points, part), BF16),
    ]
    first = call(
        lambda *refs: green_body(False, *refs), [((half_points, lanes), F32)], scratch, 40 * elements
    )(points, far_points, near_messages)[0]
    mine, told = call(
        lambda *refs: green_body(True, *refs),
        [((half_points, lanes), F32), ((half_points, lanes), BF16)],
        scratch,
        40 * elements,
    )(points, far_points, side_messages, first)
    theirs = swap(told, 2)

    def kernels(messages):
        count = line * directions
        return call(
            kernel_body,
            [((count, half_points), BF16), ((count, half_points), BF16)],
            [pltpu.VMEM((count, 8), F32), pltpu.VMEM((8, half_points), F32)],
            30 * count * half_points,
        )(points, far_points, messages[:, sources:, :])

    side_re, side_im = kernels(side_messages)
    near_re, near_im = kernels(near_messages)
    scale = 1.0 / math.sqrt(local_points * size)
    currents = call(
        lambda *refs: currents_body(scale, *refs),
        [((half_points, lanes), BF16)],
        [pltpu.VMEM((half_points, 4), F32)],
    )(mine, theirs, points, far_points)[0]

    def radiate(re, im, dtype):
        return call(radiate_body, [((line * directions, lanes), dtype)])(re, im, currents)[0]

    given = swap(radiate(side_re, side_im, BF16), 1)
    kept, sent = call(
        fold_body, [((directions, lanes), F32), (((line - 1) * directions, lanes), BF16)]
    )(radiate(near_re, near_im, F32), given)
    sent = sent.reshape(line - 1, directions, lanes)
    arrived = [swap(sent[k - 1], 4 * k, back=True) for k in range(1, line)]
    return call(finish_body, [((directions, lanes), F32)])(kept, *arrived)[0]


def solution(mesh):
    in_specs = (
        P("grp", "refl"),
        P(("grp", "refl")),
        P("refl", "grp"),
        P("grp", "refl"),
        P(("grp", "refl")),
        P(("grp", "refl")),
        P(None, "refl"),
    )
    out_specs = P("refl", "grp")
    return jax.shard_map(
        per_device, mesh=mesh, in_specs=in_specs, out_specs=out_specs, check_vma=False
    )
```

```python
import functools
import math

import jax
import jax.numpy as jnp
from jax import lax
from jax.experimental import pallas as pl
from jax.experimental.pallas import tpu as pltpu
from jax.sharding import PartitionSpec as P

RANGE_REF = 20.0
F32, BF16 = jnp.float32, jnp.bfloat16

SIN_HALF = (3.1415902835895886, -5.167407697719414, 2.544020810735872, -0.5594899090940457)
COS_HALF = (0.9999932952798736, -4.933938014977294, 4.041283824377777, -1.222127057577997)

ROUNDER = 1.5 * 2.0**23

COORDS = 5
PACK_ROWS = 16


def horner(square, terms, scale):
    total = jnp.float32(terms[-1] * scale)
    for term in terms[-2::-1]:
        total = total * square + jnp.float32(term * scale)
    return total


def circle(turns, gain):
    part = turns - ((turns + ROUNDER) - ROUNDER)
    square = part * part
    root = math.sqrt(2.0 * abs(gain))
    half_sin = part * horner(square, SIN_HALF, root)
    half_cos = horner(square, COS_HALF, 2.0 * gain / root)
    return abs(gain) - half_sin * half_sin, half_sin * half_cos


def turned(columns):
    half = columns.shape[1] // 2
    return jnp.concatenate([-columns[:, half:], columns[:, :half]], axis=1)


def pack_body(weights, feed_plane, feed_height, cosines, message):
    rows, lanes = weights.shape
    message[:rows, :] = weights[...]
    exact = jnp.concatenate([feed_plane[...], feed_height[...], cosines[...]], axis=0)
    high = exact.astype(BF16)
    rest = exact - high.astype(F32)
    middle = rest.astype(BF16)
    low = (rest - middle.astype(F32)).astype(BF16)
    pad = jnp.zeros((PACK_ROWS - 3 * COORDS, lanes), F32)
    message[rows:, :] = jnp.concatenate(
        [high.astype(F32), middle.astype(F32), low.astype(F32), pad], axis=0
    ).astype(BF16)


def points_body(plane, height, patch, points):
    lanes = points.shape[1]
    points[0:2, :] = plane[:, :lanes]
    points[2:4, :] = plane[:, lanes:]
    points[4:6, :] = height[...]
    points[6:8, :] = patch[...]


def unpack(tail):
    tail = tail.astype(F32)
    return (tail[:COORDS] + tail[COORDS : 2 * COORDS]) + tail[2 * COORDS : 3 * COORDS]


def point_rows(points, at):
    return (2 * at, 2 * at + 1, 4 + at, 6 + at)


def fill_point_columns(points, columns, base):
    lanes = points.shape[1]
    up = points[...].T
    for at in range(2):
        columns[base + at * lanes : base + (at + 1) * lanes, :] = jnp.concatenate(
            [up[:, k : k + 1] for k in point_rows(points, at)], axis=1
        )


TILE = 16
LANES = 512


def blocks(total, most):
    return [slice(at, min(at + most, total)) for at in range(0, total, most)]


def green_body(point_sets, bases, scale, *refs):
    points, messages, refs = refs[:point_sets], refs[point_sets], refs[point_sets + 1 :]
    base, outs = refs[:bases], refs[bases:-8]
    columns, rows, weights, weights_turned, even_re, even_im, odd_re, odd_im = refs[-8:]
    count, height, lanes = messages.shape
    sources = height - PACK_ROWS
    total_points = columns.shape[0]
    for at in range(point_sets):
        fill_point_columns(points[at], columns, 2 * lanes * at)
    for at in range(count):
        where = slice(at * sources, (at + 1) * sources)
        rows[0:COORDS, where] = unpack(messages[at, sources:, :])
        block = messages[at, :sources, :]
        weights[where, :] = block
        weights_turned[where, :] = turned(block)
    chunk = even_re.shape[0]

    def fill(start, green_re, green_im):
        for at in range(0, chunk, TILE):
            here = slice(start + at, start + at + TILE)
            x, y, z = columns[here, 0:1], columns[here, 1:2], columns[here, 2:3]
            for part in blocks(count * sources, LANES):
                across = x - rows[0:1, part]
                along = y - rows[1:2, part]
                height = rows[2:3, part] - z
                squared = across * across + along * along + height * height
                inverse = lax.rsqrt(squared)
                cosine, sine = circle(squared * inverse, -RANGE_REF)
                amplitude = height * (inverse * inverse)
                green_re[at : at + TILE, part] = (amplitude * cosine).astype(BF16)
                green_im[at : at + TILE, part] = (amplitude * sine).astype(BF16)

    def add_up(start, green_re, green_im):
        here = slice(start, start + chunk)
        total = jnp.dot(green_re[...], weights[...], preferred_element_type=F32) + jnp.dot(
            green_im[...], weights_turned[...], preferred_element_type=F32
        )
        if base:
            step = base[0].shape[0]
            held = base[start // step][start % step : start % step + chunk, :]
            total = (total + held) * (columns[here, 3:4] * scale)
        for out in outs:
            out[here, :] = total.astype(out.dtype)

    slots = ((even_re, even_im), (odd_re, odd_im))
    turns = total_points // chunk
    for at in range(turns + 1):
        if at < turns:
            fill(at * chunk, *slots[at % 2])
        if at > 0:
            add_up((at - 1) * chunk, *slots[(at - 1) % 2])


def kernel_body(own_points, far_points, *refs):
    groups = refs[:2]
    outs = refs[2:6]
    columns, rows = refs[6:]
    count, height, lanes = groups[0].shape
    sources = height - PACK_ROWS
    size = count * lanes
    for which, messages in enumerate(groups):
        for at in range(count):
            uv = unpack(messages[at, sources:, :])[3:5]
            normal = jnp.sqrt(1.0 - uv[0:1] * uv[0:1] - uv[1:2] * uv[1:2])
            pad = jnp.zeros((5, lanes), F32)
            base = which * size + at * lanes
            columns[base : base + lanes, :] = jnp.concatenate([uv, normal, pad], axis=0).T
    for which, points in enumerate((own_points, far_points)):
        for at in range(2):
            base = (2 * which + at) * lanes
            for k, row in enumerate(point_rows(points, at)[:3]):
                rows[k : k + 1, base : base + lanes] = points[row : row + 1, :]
    for which in range(2):
        kernel_re, kernel_im = outs[2 * which : 2 * which + 2]

        def one(at, carry):
            start = pl.multiple_of(at * TILE, TILE)
            here = pl.ds(start, TILE)
            from_ = pl.ds(pl.multiple_of(which * size + start, TILE), TILE)
            turns = (
                columns[from_, 0:1] * rows[0:1, :]
                + columns[from_, 1:2] * rows[1:2, :]
                + columns[from_, 2:3] * rows[2:3, :]
            )
            cosine, sine = circle(turns, 1.0)
            kernel_re[here, :] = cosine.astype(BF16)
            kernel_im[here, :] = sine.astype(BF16)
            return carry

        lax.fori_loop(0, size // TILE, one, 0, unroll=16)


def radiate(kernel_re, kernel_im, held):
    return jnp.dot(kernel_re[...], held, preferred_element_type=F32) + jnp.dot(
        kernel_im[...], turned(held), preferred_element_type=F32
    )


def side_body(mine, theirs, kernel_re, kernel_im, currents, out):
    half = mine.shape[0] // 2
    for here, there in ((slice(0, half), slice(half, None)), (slice(half, None), slice(0, half))):
        currents[here, :] = (mine[here, :] + theirs[there, :].astype(F32)).astype(BF16)
    out[...] = radiate(kernel_re, kernel_im, currents[...]).astype(out.dtype)


def near_body(currents, kernel_re, kernel_im, out):
    out[...] = radiate(kernel_re, kernel_im, currents[...])


def fold_body(mine, theirs, kept, sent):
    first = kept.shape[0]
    total = mine[...] + theirs[...].astype(F32)
    kept[...] = total[:first]
    sent[...] = total[first:].astype(BF16)


def finish_body(kept, *refs):
    total = kept[...]
    for ref in refs[:-1]:
        total = total + ref[...].astype(F32)
    refs[-1][...] = total


def call(body, outs, scratch=(), flops=0, moved=0):
    return pl.pallas_call(
        body,
        out_shape=[jax.ShapeDtypeStruct(*out) for out in outs],
        scratch_shapes=list(scratch),
        compiler_params=pltpu.CompilerParams(vmem_limit_bytes=32 * 1024 * 1024),
        cost_estimate=pl.CostEstimate(flops=flops, bytes_accessed=moved, transcendentals=0),
    )


def per_device(
    feed_plane,
    feed_height,
    feed_weights,
    point_plane,
    point_height,
    patch_factor,
    direction_cosines,
):
    size = lax.axis_size("refl")
    line = size // 4
    sources, lanes = feed_weights.shape
    local_points = point_height.shape[0]
    half_points = 2 * local_points
    directions = direction_cosines.shape[1]

    def pairs(step):
        out = []
        for at in range(size):
            row, place = divmod(at, 4)
            far, near = divmod(step, 4)
            to = (row ^ far) if line & (line - 1) == 0 else (row + far) % line
            out.append((at, to * 4 + (place ^ near)))
        return out

    def swap(x, step, back=False):
        links = pairs(step)
        return lax.ppermute(x, "refl", [(b, a) for a, b in links] if back else links)

    message = call(pack_body, [((sources + PACK_ROWS, lanes), BF16)])(
        feed_weights, feed_plane, feed_height.reshape(1, lanes), direction_cosines
    )[0]
    points = call(points_body, [((8, lanes), F32)])(
        point_plane, point_height.reshape(2, lanes), patch_factor.reshape(2, lanes)
    )[0]
    arrived = [swap(message, 4 * k + 1) for k in range(1, line)]
    far_points = swap(points, 3)
    near_messages = jnp.stack([message, *arrived])
    side_messages = jnp.stack([swap(x, 1) for x in [message, *arrived]])

    part = line * sources
    chunk = local_points // 2
    scale = 1.0 / math.sqrt(local_points * size)

    def green(points, messages, bases, types):
        rows = len(points) * local_points
        scratch = [
            pltpu.VMEM((rows, 4), F32),
            pltpu.VMEM((8, part), F32),
            pltpu.VMEM((part, lanes), BF16),
            pltpu.VMEM((part, lanes), BF16),
        ] + [pltpu.VMEM((chunk, part), BF16)] * 4
        return call(
            functools.partial(green_body, len(points), len(bases), scale),
            [((rows, lanes), kind) for kind in types],
            scratch,
            0,
        )(*points, messages, *bases)

    bases = [green([which], near_messages, [], [F32])[0] for which in (points, far_points)]
    mine, told = green([points, far_points], side_messages, bases, [F32, BF16])
    theirs = swap(told, 3)

    count = line * directions
    near_re, near_im, side_re, side_im = call(
        kernel_body,
        [((count, half_points), BF16)] * 4,
        [pltpu.VMEM((2 * count, 8), F32), pltpu.VMEM((8, half_points), F32)],
        60 * count * half_points,
    )(points, far_points, near_messages, side_messages)
    currents, told = call(side_body, [((half_points, lanes), BF16), ((count, lanes), BF16)])(
        mine, theirs, side_re, side_im
    )
    given = swap(told, 1)
    near = call(near_body, [((count, lanes), F32)])(currents, near_re, near_im)[0]
    kept, sent = call(
        fold_body, [((directions, lanes), F32), (((line - 1) * directions, lanes), BF16)]
    )(near, given)
    sent = sent.reshape(line - 1, directions, lanes)
    arrived = [swap(sent[k - 1], 4 * k + 1, back=True) for k in range(1, line)]
    return call(finish_body, [((directions, lanes), F32)])(kept, *arrived)[0]


def solution(mesh):
    in_specs = (
        P("grp", "refl"),
        P(("grp", "refl")),
        P("refl", "grp"),
        P("grp", "refl"),
        P(("grp", "refl")),
        P(("grp", "refl")),
        P(None, "refl"),
    )
    out_specs = P("refl", "grp")
    return jax.shard_map(
        per_device, mesh=mesh, in_specs=in_specs, out_specs=out_specs, check_vma=False
    )
```

```python
import functools
import math

import jax
import jax.numpy as jnp
from jax import lax
from jax.experimental import pallas as pl
from jax.experimental.pallas import tpu as pltpu
from jax.sharding import PartitionSpec as P

RANGE_REF = 20.0
F32, BF16 = jnp.float32, jnp.bfloat16

SIN_HALF = (3.1415902835895886, -5.167407697719414, 2.544020810735872, -0.5594899090940457)
COS_HALF = (0.9999932952798736, -4.933938014977294, 4.041283824377777, -1.222127057577997)

ROUNDER = 1.5 * 2.0**23

COORDS = 5
PACK_ROWS = 16


def horner(square, terms, scale):
    total = jnp.float32(terms[-1] * scale)
    for term in terms[-2::-1]:
        total = total * square + jnp.float32(term * scale)
    return total


def circle(turns, gain):
    part = turns - ((turns + ROUNDER) - ROUNDER)
    square = part * part
    root = math.sqrt(2.0 * abs(gain))
    half_sin = part * horner(square, SIN_HALF, root)
    half_cos = horner(square, COS_HALF, 2.0 * gain / root)
    return abs(gain) - half_sin * half_sin, half_sin * half_cos


def turned(columns):
    half = columns.shape[1] // 2
    return jnp.concatenate([-columns[:, half:], columns[:, :half]], axis=1)


def pack_body(
    weights, feed_plane, feed_height, cosines, plane, height, patch, message, points, coords, ends, sems
):
    rows, lanes = weights.shape
    sources = [feed_plane, feed_height, cosines, plane, height, patch, weights]
    targets = [
        coords.at[0:2, :],
        coords.at[2:3, :],
        coords.at[3:5, :],
        ends,
        points.at[4:6, :],
        points.at[6:8, :],
        message.at[0:rows, :],
    ]
    copies = [
        pltpu.make_async_copy(source, target, sems.at[at])
        for at, (source, target) in enumerate(zip(sources, targets))
    ]
    for copy in copies:
        copy.start()
    for copy in copies[:4]:
        copy.wait()
    points[0:2, :] = ends[:, :lanes]
    points[2:4, :] = ends[:, lanes:]
    exact = coords[0:COORDS, :]
    high = exact.astype(BF16)
    rest = exact - high.astype(F32)
    middle = rest.astype(BF16)
    low = (rest - middle.astype(F32)).astype(BF16)
    pad = jnp.zeros((PACK_ROWS - 3 * COORDS, lanes), F32)
    message[rows:, :] = jnp.concatenate(
        [high.astype(F32), middle.astype(F32), low.astype(F32), pad], axis=0
    ).astype(BF16)
    for copy in copies[4:]:
        copy.wait()


def unpack(tail):
    tail = tail.astype(F32)
    return (tail[:COORDS] + tail[COORDS : 2 * COORDS]) + tail[2 * COORDS : 3 * COORDS]


def point_rows(points, at):
    return (2 * at, 2 * at + 1, 4 + at, 6 + at)


def fill_point_columns(points, columns, base):
    lanes = points.shape[1]
    up = points[...].T
    for at in range(2):
        columns[base + at * lanes : base + (at + 1) * lanes, :] = jnp.concatenate(
            [up[:, k : k + 1] for k in point_rows(points, at)], axis=1
        )


TILE = 16
LANES = 512


def blocks(total, most):
    return [slice(at, min(at + most, total)) for at in range(0, total, most)]


def green_body(point_sets, bases, scale, *refs):
    points, messages, refs = refs[:point_sets], refs[point_sets], refs[point_sets + 1 :]
    base, outs = refs[:bases], refs[bases:-8]
    columns, rows, weights, weights_turned, even_re, even_im, odd_re, odd_im = refs[-8:]
    count, height, lanes = messages.shape
    sources = height - PACK_ROWS
    total_points = columns.shape[0]
    for at in range(point_sets):
        fill_point_columns(points[at], columns, 2 * lanes * at)
    for at in range(count):
        where = slice(at * sources, (at + 1) * sources)
        rows[0:COORDS, where] = unpack(messages[at, sources:, :])
        block = messages[at, :sources, :]
        weights[where, :] = block
        weights_turned[where, :] = turned(block)
    chunk = even_re.shape[0]

    def fill(start, green_re, green_im):
        for at in range(0, chunk, TILE):
            here = slice(start + at, start + at + TILE)
            x, y, z = columns[here, 0:1], columns[here, 1:2], columns[here, 2:3]
            for part in blocks(count * sources, LANES):
                across = x - rows[0:1, part]
                along = y - rows[1:2, part]
                height = rows[2:3, part] - z
                squared = across * across + along * along + height * height
                inverse = lax.rsqrt(squared)
                cosine, sine = circle(squared * inverse, -RANGE_REF)
                amplitude = height * (inverse * inverse)
                green_re[at : at + TILE, part] = (amplitude * cosine).astype(BF16)
                green_im[at : at + TILE, part] = (amplitude * sine).astype(BF16)

    def add_up(start, green_re, green_im):
        here = slice(start, start + chunk)
        total = jnp.dot(green_re[...], weights[...], preferred_element_type=F32) + jnp.dot(
            green_im[...], weights_turned[...], preferred_element_type=F32
        )
        if base:
            step = base[0].shape[0]
            held = base[start // step][start % step : start % step + chunk, :]
            total = (total + held) * (columns[here, 3:4] * scale)
        for out in outs:
            out[here, :] = total.astype(out.dtype)

    slots = ((even_re, even_im), (odd_re, odd_im))
    turns = total_points // chunk
    for at in range(turns + 1):
        if at < turns:
            fill(at * chunk, *slots[at % 2])
        if at > 0:
            add_up((at - 1) * chunk, *slots[(at - 1) % 2])


def kernel_body(own_points, far_points, *refs):
    groups = refs[:2]
    outs = refs[2:6]
    columns, rows = refs[6:]
    count, height, lanes = groups[0].shape
    sources = height - PACK_ROWS
    size = count * lanes
    for which, messages in enumerate(groups):
        for at in range(count):
            uv = unpack(messages[at, sources:, :])[3:5]
            normal = jnp.sqrt(1.0 - uv[0:1] * uv[0:1] - uv[1:2] * uv[1:2])
            pad = jnp.zeros((5, lanes), F32)
            base = which * size + at * lanes
            columns[base : base + lanes, :] = jnp.concatenate([uv, normal, pad], axis=0).T
    for which, points in enumerate((own_points, far_points)):
        for at in range(2):
            base = (2 * which + at) * lanes
            for k, row in enumerate(point_rows(points, at)[:3]):
                rows[k : k + 1, base : base + lanes] = points[row : row + 1, :]
    for which in range(2):
        kernel_re, kernel_im = outs[2 * which : 2 * which + 2]

        def one(at, carry):
            start = pl.multiple_of(at * TILE, TILE)
            here = pl.ds(start, TILE)
            from_ = pl.ds(pl.multiple_of(which * size + start, TILE), TILE)
            turns = (
                columns[from_, 0:1] * rows[0:1, :]
                + columns[from_, 1:2] * rows[1:2, :]
                + columns[from_, 2:3] * rows[2:3, :]
            )
            cosine, sine = circle(turns, 1.0)
            kernel_re[here, :] = cosine.astype(BF16)
            kernel_im[here, :] = sine.astype(BF16)
            return carry

        lax.fori_loop(0, size // TILE, one, 0, unroll=16)


def radiate(kernel_re, kernel_im, held):
    return jnp.dot(kernel_re[...], held, preferred_element_type=F32) + jnp.dot(
        kernel_im[...], turned(held), preferred_element_type=F32
    )


def side_body(mine, theirs, kernel_re, kernel_im, currents, out):
    half = mine.shape[0] // 2
    for here, there in ((slice(0, half), slice(half, None)), (slice(half, None), slice(0, half))):
        currents[here, :] = (mine[here, :] + theirs[there, :].astype(F32)).astype(BF16)
    out[...] = radiate(kernel_re, kernel_im, currents[...]).astype(out.dtype)


def near_body(currents, kernel_re, kernel_im, out):
    out[...] = radiate(kernel_re, kernel_im, currents[...])


def fold_body(mine, theirs, kept, sent):
    first = kept.shape[0]
    total = mine[...] + theirs[...].astype(F32)
    kept[...] = total[:first]
    sent[...] = total[first:].astype(BF16)


def finish_body(kept, *refs):
    total = kept[...]
    for ref in refs[:-1]:
        total = total + ref[...].astype(F32)
    refs[-1][...] = total


def call(body, outs, scratch=(), flops=0, anywhere=0, room=32 << 20):
    places = [pl.BlockSpec(memory_space=pltpu.HBM)] * anywhere
    return pl.pallas_call(
        body,
        out_shape=[jax.ShapeDtypeStruct(*out) for out in outs],
        scratch_shapes=list(scratch),
        compiler_params=pltpu.CompilerParams(vmem_limit_bytes=room),
        cost_estimate=pl.CostEstimate(flops=flops, bytes_accessed=0, transcendentals=0),
        **(dict(in_specs=places) if anywhere else {}),
    )


def per_device(
    feed_plane,
    feed_height,
    feed_weights,
    point_plane,
    point_height,
    patch_factor,
    direction_cosines,
):
    size = lax.axis_size("refl")
    line = size // 4
    sources, lanes = feed_weights.shape
    local_points = point_height.shape[0]
    half_points = 2 * local_points
    directions = direction_cosines.shape[1]

    def pairs(step):
        out = []
        for at in range(size):
            row, place = divmod(at, 4)
            far, near = divmod(step, 4)
            to = (row ^ far) if line & (line - 1) == 0 else (row + far) % line
            out.append((at, to * 4 + (place ^ near)))
        return out

    def swap(x, step, back=False):
        links = pairs(step)
        return lax.ppermute(x, "refl", [(b, a) for a, b in links] if back else links)

    message, points = call(
        pack_body,
        [((sources + PACK_ROWS, lanes), BF16), ((8, lanes), F32)],
        [pltpu.VMEM((8, lanes), F32), pltpu.VMEM((2, 2 * lanes), F32), pltpu.SemaphoreType.DMA((7,))],
        anywhere=7,
        room=32 << 20,
    )(
        *[
            pltpu.with_memory_space_constraint(x, pltpu.HBM)
            for x in (
                feed_weights,
                feed_plane,
                feed_height.reshape(1, lanes),
                direction_cosines,
                point_plane,
                point_height.reshape(2, lanes),
                patch_factor.reshape(2, lanes),
            )
        ]
    )
    arrived = [swap(message, 4 * k + 1) for k in range(1, line)]
    far_points = swap(points, 3)
    far_points, *arrived = lax.optimization_barrier((far_points, *arrived))
    near_messages = jnp.stack([message, *arrived])
    side_messages = swap(near_messages, 1)

    part = line * sources
    chunk = local_points // 2
    scale = 1.0 / math.sqrt(local_points * size)

    def green(points, messages, bases, types):
        rows = len(points) * local_points
        scratch = [
            pltpu.VMEM((rows, 4), F32),
            pltpu.VMEM((8, part), F32),
            pltpu.VMEM((part, lanes), BF16),
            pltpu.VMEM((part, lanes), BF16),
        ] + [pltpu.VMEM((chunk, part), BF16)] * 4
        return call(
            functools.partial(green_body, len(points), len(bases), scale),
            [((rows, lanes), kind) for kind in types],
            scratch,
            0,
        )(*points, messages, *bases)

    sets = [points, far_points]
    bases = green(sets, near_messages, [], [F32])
    mine, told = green(sets, side_messages, bases, [F32, BF16])
    theirs = swap(told, 3)

    count = line * directions
    near_re, near_im, side_re, side_im = call(
        kernel_body,
        [((count, half_points), BF16)] * 4,
        [pltpu.VMEM((2 * count, 8), F32), pltpu.VMEM((8, half_points), F32)],
        60 * count * half_points,
    )(points, far_points, near_messages, side_messages)
    currents, told = call(side_body, [((half_points, lanes), BF16), ((count, lanes), BF16)])(
        mine, theirs, side_re, side_im
    )
    given = swap(told, 1)
    near = call(near_body, [((count, lanes), F32)])(currents, near_re, near_im)[0]
    kept, sent = call(
        fold_body, [((directions, lanes), F32), (((line - 1) * directions, lanes), BF16)]
    )(near, given)
    sent = sent.reshape(line - 1, directions, lanes)
    arrived = [swap(sent[k - 1], 4 * k + 1, back=True) for k in range(1, line)]
    return call(finish_body, [((directions, lanes), F32)])(kept, *arrived)[0]


def solution(mesh):
    in_specs = (
        P("grp", "refl"),
        P(("grp", "refl")),
        P("refl", "grp"),
        P("grp", "refl"),
        P(("grp", "refl")),
        P(("grp", "refl")),
        P(None, "refl"),
    )
    out_specs = P("refl", "grp")
    return jax.shard_map(
        per_device, mesh=mesh, in_specs=in_specs, out_specs=out_specs, check_vma=False
    )
```

```python
import functools
import math

import jax
import jax.numpy as jnp
from jax import lax
from jax.experimental import pallas as pl
from jax.experimental.pallas import tpu as pltpu
from jax.sharding import PartitionSpec as P

RANGE_REF = 20.0
F32, BF16 = jnp.float32, jnp.bfloat16

SIN_HALF = (3.1415902835895886, -5.167407697719414, 2.544020810735872, -0.5594899090940457)
COS_HALF = (0.9999932952798736, -4.933938014977294, 4.041283824377777, -1.222127057577997)

ROUNDER = 1.5 * 2.0**23

TERMS = 32
MIDDLE = 22.0

COORDS = 5
PACK_ROWS = 16


def horner(square, terms, scale):
    total = jnp.float32(terms[-1] * scale)
    for term in terms[-2::-1]:
        total = total * square + jnp.float32(term * scale)
    return total


def circle(turns, gain):
    part = turns - ((turns + ROUNDER) - ROUNDER)
    square = part * part
    root = math.sqrt(2.0 * abs(gain))
    half_sin = part * horner(square, SIN_HALF, root)
    half_cos = horner(square, COS_HALF, 2.0 * gain / root)
    return abs(gain) - half_sin * half_sin, half_sin * half_cos


def turned(columns):
    half = columns.shape[1] // 2
    return jnp.concatenate([-columns[:, half:], columns[:, :half]], axis=1)


def pack_body(
    weights, feed_plane, feed_height, cosines, plane, height, patch, message, points, coords, ends, sems
):
    rows, lanes = weights.shape
    sources = [feed_plane, feed_height, cosines, plane, height, patch, weights]
    targets = [
        coords.at[0:2, :],
        coords.at[2:3, :],
        coords.at[3:5, :],
        ends,
        points.at[4:6, :],
        points.at[6:8, :],
        message.at[0:rows, :],
    ]
    copies = [
        pltpu.make_async_copy(source, target, sems.at[at])
        for at, (source, target) in enumerate(zip(sources, targets))
    ]
    for copy in copies:
        copy.start()
    for copy in copies[:4]:
        copy.wait()
    points[0:2, :] = ends[:, :lanes]
    points[2:4, :] = ends[:, lanes:]
    exact = coords[0:COORDS, :]
    high = exact.astype(BF16)
    rest = exact - high.astype(F32)
    middle = rest.astype(BF16)
    low = (rest - middle.astype(F32)).astype(BF16)
    pad = jnp.zeros((PACK_ROWS - 3 * COORDS, lanes), F32)
    message[rows:, :] = jnp.concatenate(
        [high.astype(F32), middle.astype(F32), low.astype(F32), pad], axis=0
    ).astype(BF16)
    for copy in copies[4:]:
        copy.wait()


def unpack(tail):
    tail = tail.astype(F32)
    return (tail[:COORDS] + tail[COORDS : 2 * COORDS]) + tail[2 * COORDS : 3 * COORDS]


def split(value):
    high = value.astype(BF16).astype(F32)
    rest = value - high
    middle = rest.astype(BF16).astype(F32)
    return high, middle, (rest - middle).astype(BF16).astype(F32)


def distance_terms(x, y, z, is_point):
    z = z - MIDDLE
    square = x * x + y * y + z * z
    out = []
    for value in (x, y, z):
        high, middle, low = split(value if is_point else -2.0 * value)
        out += [high, high, middle, high, middle, low] if is_point else [high, middle, high, low, middle, high]
    ones = [jnp.ones_like(x)] * 3
    out += list(split(square)) + ones if is_point else ones + list(split(square))
    return jnp.concatenate(out + [jnp.zeros_like(x)] * (TERMS - len(out)), axis=0)


def point_rows(points, at):
    return (2 * at, 2 * at + 1, 4 + at, 6 + at)


def fill_point_columns(points, columns, base):
    lanes = points.shape[1]
    up = points[...].T
    for at in range(2):
        columns[base + at * lanes : base + (at + 1) * lanes, :] = jnp.concatenate(
            [up[:, k : k + 1] for k in point_rows(points, at)], axis=1
        )


TILE = 32
LANES = 512


def blocks(total, most):
    return [slice(at, min(at + most, total)) for at in range(0, total, most)]


def green_body(point_sets, bases, scale, *refs):
    points, messages, refs = refs[:point_sets], refs[point_sets], refs[point_sets + 1 :]
    base, outs = refs[:bases], refs[bases:-12]
    columns, left, heights, right, weights, weights_turned, *slots = refs[-12:]
    slots = (slots[:3], slots[3:])
    count, height, lanes = messages.shape
    sources = height - PACK_ROWS
    total_points = columns.shape[0]
    for at in range(point_sets):
        fill_point_columns(points[at], columns, 2 * lanes * at)
        for half in range(2):
            x, y, z = (points[at][k : k + 1, :] for k in point_rows(points[at], half)[:3])
            start = (2 * at + half) * lanes
            left[start : start + lanes, :] = distance_terms(x, y, z, True).T.astype(BF16)
    for at in range(count):
        where = slice(at * sources, (at + 1) * sources)
        coords = unpack(messages[at, sources:, :])
        x, y, z = coords[0:1], coords[1:2], coords[2:3]
        heights[0:1, where] = z
        right[:, where] = distance_terms(x, y, z, False).astype(BF16)
        block = messages[at, :sources, :]
        weights[where, :] = block
        weights_turned[where, :] = turned(block)
    chunk = slots[0][0].shape[0]

    def fill(start, green_re, green_im, squares):
        squares[...] = jnp.dot(
            left[start : start + chunk, :], right[...], preferred_element_type=F32
        )
        for at in range(0, chunk, TILE):
            low = columns[start + at : start + at + TILE, 2:3]
            for part in blocks(count * sources, LANES):
                squared = squares[at : at + TILE, part]
                inverse = lax.rsqrt(squared)
                cosine, sine = circle(squared * inverse, -RANGE_REF)
                amplitude = (heights[0:1, part] - low) * (inverse * inverse)
                green_re[at : at + TILE, part] = (amplitude * cosine).astype(BF16)
                green_im[at : at + TILE, part] = (amplitude * sine).astype(BF16)

    def add_up(start, green_re, green_im, _):
        here = slice(start, start + chunk)
        total = jnp.dot(green_re[...], weights[...], preferred_element_type=F32) + jnp.dot(
            green_im[...], weights_turned[...], preferred_element_type=F32
        )
        if base:
            step = base[0].shape[0]
            held = base[start // step][start % step : start % step + chunk, :]
            total = (total + held) * (columns[here, 3:4] * scale)
        for out in outs:
            out[here, :] = total.astype(out.dtype)

    turns = total_points // chunk
    for at in range(turns + 1):
        if at < turns:
            fill(at * chunk, *slots[at % 2])
        if at > 0:
            add_up((at - 1) * chunk, *slots[(at - 1) % 2])


def kernel_body(own_points, far_points, *refs):
    groups = refs[:2]
    outs = refs[2:6]
    columns, rows = refs[6:]
    count, height, lanes = groups[0].shape
    sources = height - PACK_ROWS
    size = count * lanes
    for which, messages in enumerate(groups):
        for at in range(count):
            uv = unpack(messages[at, sources:, :])[3:5]
            normal = jnp.sqrt(1.0 - uv[0:1] * uv[0:1] - uv[1:2] * uv[1:2])
            pad = jnp.zeros((5, lanes), F32)
            base = which * size + at * lanes
            columns[base : base + lanes, :] = jnp.concatenate([uv, normal, pad], axis=0).T
    for which, points in enumerate((own_points, far_points)):
        for at in range(2):
            base = (2 * which + at) * lanes
            for k, row in enumerate(point_rows(points, at)[:3]):
                rows[k : k + 1, base : base + lanes] = points[row : row + 1, :]
    for which in range(2):
        kernel_re, kernel_im = outs[2 * which : 2 * which + 2]

        def one(at, carry):
            start = pl.multiple_of(at * TILE, TILE)
            here = pl.ds(start, TILE)
            from_ = pl.ds(pl.multiple_of(which * size + start, TILE), TILE)
            turns = (
                columns[from_, 0:1] * rows[0:1, :]
                + columns[from_, 1:2] * rows[1:2, :]
                + columns[from_, 2:3] * rows[2:3, :]
            )
            cosine, sine = circle(turns, 1.0)
            kernel_re[here, :] = cosine.astype(BF16)
            kernel_im[here, :] = sine.astype(BF16)
            return carry

        lax.fori_loop(0, size // TILE, one, 0, unroll=16)


def radiate(kernel_re, kernel_im, held):
    return jnp.dot(kernel_re[...], held, preferred_element_type=F32) + jnp.dot(
        kernel_im[...], turned(held), preferred_element_type=F32
    )


def side_body(mine, theirs, kernel_re, kernel_im, currents, out):
    half = mine.shape[0] // 2
    for here, there in ((slice(0, half), slice(half, None)), (slice(half, None), slice(0, half))):
        currents[here, :] = (mine[here, :] + theirs[there, :].astype(F32)).astype(BF16)
    out[...] = radiate(kernel_re, kernel_im, currents[...]).astype(out.dtype)


def near_body(currents, kernel_re, kernel_im, out):
    out[...] = radiate(kernel_re, kernel_im, currents[...])


def fold_body(mine, theirs, kept, sent):
    first = kept.shape[0]
    total = mine[...] + theirs[...].astype(F32)
    kept[...] = total[:first]
    sent[...] = total[first:].astype(BF16)


def finish_body(kept, *refs):
    total = kept[...]
    for ref in refs[:-1]:
        total = total + ref[...].astype(F32)
    refs[-1][...] = total


def call(body, outs, scratch=(), flops=0, anywhere=0, room=32 << 20):
    places = [pl.BlockSpec(memory_space=pltpu.HBM)] * anywhere
    return pl.pallas_call(
        body,
        out_shape=[jax.ShapeDtypeStruct(*out) for out in outs],
        scratch_shapes=list(scratch),
        compiler_params=pltpu.CompilerParams(vmem_limit_bytes=room),
        cost_estimate=pl.CostEstimate(flops=flops, bytes_accessed=0, transcendentals=0),
        **(dict(in_specs=places) if anywhere else {}),
    )


def per_device(
    feed_plane,
    feed_height,
    feed_weights,
    point_plane,
    point_height,
    patch_factor,
    direction_cosines,
):
    size = lax.axis_size("refl")
    line = size // 4
    sources, lanes = feed_weights.shape
    local_points = point_height.shape[0]
    half_points = 2 * local_points
    directions = direction_cosines.shape[1]

    def pairs(step):
        out = []
        for at in range(size):
            row, place = divmod(at, 4)
            far, near = divmod(step, 4)
            to = (row ^ far) if line & (line - 1) == 0 else (row + far) % line
            out.append((at, to * 4 + (place ^ near)))
        return out

    def swap(x, step, back=False):
        links = pairs(step)
        return lax.ppermute(x, "refl", [(b, a) for a, b in links] if back else links)

    message, points = call(
        pack_body,
        [((sources + PACK_ROWS, lanes), BF16), ((8, lanes), F32)],
        [pltpu.VMEM((8, lanes), F32), pltpu.VMEM((2, 2 * lanes), F32), pltpu.SemaphoreType.DMA((7,))],
        anywhere=7,
        room=32 << 20,
    )(
        *[
            pltpu.with_memory_space_constraint(x, pltpu.HBM)
            for x in (
                feed_weights,
                feed_plane,
                feed_height.reshape(1, lanes),
                direction_cosines,
                point_plane,
                point_height.reshape(2, lanes),
                patch_factor.reshape(2, lanes),
            )
        ]
    )
    arrived = [swap(message, 4 * k + 1) for k in range(1, line)]
    far_points = swap(points, 3)
    far_points, *arrived = lax.optimization_barrier((far_points, *arrived))
    near_messages = jnp.stack([message, *arrived])
    side_messages = swap(near_messages, 1)

    part = line * sources
    chunk = local_points
    scale = 1.0 / math.sqrt(local_points * size)

    def green(points, messages, bases, types):
        rows = len(points) * local_points
        slot = [((chunk, part), BF16), ((chunk, part), BF16), ((chunk, part), F32)]
        scratch = [
            ((rows, 4), F32),
            ((rows, TERMS), BF16),
            ((8, part), F32),
            ((TERMS, part), BF16),
            ((part, lanes), BF16),
            ((part, lanes), BF16),
            *slot,
            *slot,
        ]
        scratch = [pltpu.VMEM(*which) for which in scratch]
        return call(
            functools.partial(green_body, len(points), len(bases), scale),
            [((rows, lanes), kind) for kind in types],
            scratch,
            0,
        )(*points, messages, *bases)

    sets = [points, far_points]
    bases = green(sets, near_messages, [], [F32])
    mine, told = green(sets, side_messages, bases, [F32, BF16])
    theirs = swap(told, 3)

    count = line * directions
    near_re, near_im, side_re, side_im = call(
        kernel_body,
        [((count, half_points), BF16)] * 4,
        [pltpu.VMEM((2 * count, 8), F32), pltpu.VMEM((8, half_points), F32)],
        60 * count * half_points,
    )(points, far_points, near_messages, side_messages)
    currents, told = call(side_body, [((half_points, lanes), BF16), ((count, lanes), BF16)])(
        mine, theirs, side_re, side_im
    )
    given = swap(told, 1)
    near = call(near_body, [((count, lanes), F32)])(currents, near_re, near_im)[0]
    kept, sent = call(
        fold_body, [((directions, lanes), F32), (((line - 1) * directions, lanes), BF16)]
    )(near, given)
    sent = sent.reshape(line - 1, directions, lanes)
    arrived = [swap(sent[k - 1], 4 * k + 1, back=True) for k in range(1, line)]
    return call(finish_body, [((directions, lanes), F32)])(kept, *arrived)[0]


def solution(mesh):
    in_specs = (
        P("grp", "refl"),
        P(("grp", "refl")),
        P("refl", "grp"),
        P("grp", "refl"),
        P(("grp", "refl")),
        P(("grp", "refl")),
        P(None, "refl"),
    )
    out_specs = P("refl", "grp")
    return jax.shard_map(
        per_device, mesh=mesh, in_specs=in_specs, out_specs=out_specs, check_vma=False
    )
```

```python
import functools
import math

import jax
import jax.numpy as jnp
from jax import lax
from jax.experimental import pallas as pl
from jax.experimental.pallas import tpu as pltpu
from jax.sharding import PartitionSpec as P

RANGE_REF = 20.0
F32, BF16 = jnp.float32, jnp.bfloat16

SIN_HALF = (3.1415902835895886, -5.167407697719414, 2.544020810735872, -0.5594899090940457)
COS_HALF = (0.9999932952798736, -4.933938014977294, 4.041283824377777, -1.222127057577997)

ROUNDER = 1.5 * 2.0**23

TERMS = 32
MIDDLE = 22.0

COORDS = 5
PACK_ROWS = 16


def horner(square, terms, scale):
    total = jnp.float32(terms[-1] * scale)
    for term in terms[-2::-1]:
        total = total * square + jnp.float32(term * scale)
    return total


def circle(turns, gain):
    part = turns - ((turns + ROUNDER) - ROUNDER)
    square = part * part
    root = math.sqrt(2.0 * abs(gain))
    half_sin = part * horner(square, SIN_HALF, root)
    half_cos = horner(square, COS_HALF, 2.0 * gain / root)
    return abs(gain) - half_sin * half_sin, half_sin * half_cos


def turned(columns):
    half = columns.shape[1] // 2
    return jnp.concatenate([-columns[:, half:], columns[:, :half]], axis=1)


def pack_body(
    weights, feed_plane, feed_height, cosines, plane, height, patch, message, points, coords, ends, sems
):
    rows, lanes = weights.shape
    sources = [feed_plane, feed_height, cosines, plane, height, patch, weights]
    targets = [
        coords.at[0:2, :],
        coords.at[2:3, :],
        coords.at[3:5, :],
        ends,
        points.at[4:6, :],
        points.at[6:8, :],
        message.at[0:rows, :],
    ]
    copies = [
        pltpu.make_async_copy(source, target, sems.at[at])
        for at, (source, target) in enumerate(zip(sources, targets))
    ]
    for copy in copies[::-1]:
        copy.start()
    for copy in copies[:4]:
        copy.wait()
    points[0:2, :] = ends[:, :lanes]
    points[2:4, :] = ends[:, lanes:]
    exact = coords[0:COORDS, :]
    high = exact.astype(BF16)
    rest = exact - high.astype(F32)
    middle = rest.astype(BF16)
    low = (rest - middle.astype(F32)).astype(BF16)
    pad = jnp.zeros((PACK_ROWS - 3 * COORDS, lanes), F32)
    message[rows:, :] = jnp.concatenate(
        [high.astype(F32), middle.astype(F32), low.astype(F32), pad], axis=0
    ).astype(BF16)
    for copy in copies[4:]:
        copy.wait()


def unpack(tail):
    tail = tail.astype(F32)
    return (tail[:COORDS] + tail[COORDS : 2 * COORDS]) + tail[2 * COORDS : 3 * COORDS]


def split(value):
    high = value.astype(BF16).astype(F32)
    rest = value - high
    middle = rest.astype(BF16).astype(F32)
    return high, middle, (rest - middle).astype(BF16).astype(F32)


def distance_terms(x, y, z, is_point):
    z = z - MIDDLE
    square = x * x + y * y + z * z
    out = []
    for value in (x, y, z):
        high, middle, low = split(value if is_point else -2.0 * value)
        out += [high, high, middle, high, middle, low] if is_point else [high, middle, high, low, middle, high]
    ones = [jnp.ones_like(x)] * 3
    out += list(split(square)) + ones if is_point else ones + list(split(square))
    return jnp.concatenate(out + [jnp.zeros_like(x)] * (TERMS - len(out)), axis=0)


def point_rows(points, at):
    return (2 * at, 2 * at + 1, 4 + at, 6 + at)


def fill_point_columns(points, columns, base):
    lanes = points.shape[1]
    up = points[...].T
    for at in range(2):
        columns[base + at * lanes : base + (at + 1) * lanes, :] = jnp.concatenate(
            [up[:, k : k + 1] for k in point_rows(points, at)], axis=1
        )


TILE = 32
LANES = 512


def blocks(total, most):
    return [slice(at, min(at + most, total)) for at in range(0, total, most)]


def green_body(point_sets, bases, scale, *refs):
    points, messages, refs = refs[:point_sets], refs[point_sets], refs[point_sets + 1 :]
    base, outs = refs[:bases], refs[bases:-12]
    columns, left, heights, right, weights, weights_turned, *slots = refs[-12:]
    slots = (slots[:3], slots[3:])
    count, height, lanes = messages.shape
    sources = height - PACK_ROWS
    total_points = columns.shape[0]
    for at in range(point_sets):
        fill_point_columns(points[at], columns, 2 * lanes * at)
        for half in range(2):
            x, y, z = (points[at][k : k + 1, :] for k in point_rows(points[at], half)[:3])
            start = (2 * at + half) * lanes
            left[start : start + lanes, :] = distance_terms(x, y, z, True).T.astype(BF16)
    for at in range(count):
        where = slice(at * sources, (at + 1) * sources)
        coords = unpack(messages[at, sources:, :])
        x, y, z = coords[0:1], coords[1:2], coords[2:3]
        heights[0:1, where] = z
        right[:, where] = distance_terms(x, y, z, False).astype(BF16)
        block = messages[at, :sources, :]
        weights[where, :] = block
        weights_turned[where, :] = turned(block)
    chunk = slots[0][0].shape[0]

    def fill(start, green_re, green_im, squares):
        squares[...] = jnp.dot(
            left[start : start + chunk, :], right[...], preferred_element_type=F32
        )
        for at in range(0, chunk, TILE):
            low = columns[start + at : start + at + TILE, 2:3]
            for part in blocks(count * sources, LANES):
                squared = squares[at : at + TILE, part]
                inverse = lax.rsqrt(squared)
                cosine, sine = circle(squared * inverse, -RANGE_REF)
                amplitude = (heights[0:1, part] - low) * (inverse * inverse)
                green_re[at : at + TILE, part] = (amplitude * cosine).astype(BF16)
                green_im[at : at + TILE, part] = (amplitude * sine).astype(BF16)

    def add_up(start, green_re, green_im, _):
        here = slice(start, start + chunk)
        total = jnp.dot(green_re[...], weights[...], preferred_element_type=F32) + jnp.dot(
            green_im[...], weights_turned[...], preferred_element_type=F32
        )
        if base:
            step = base[0].shape[0]
            held = base[start // step][start % step : start % step + chunk, :]
            total = (total + held) * (columns[here, 3:4] * scale)
        for out in outs:
            out[here, :] = total.astype(out.dtype)

    turns = total_points // chunk
    for at in range(turns + 1):
        if at < turns:
            fill(at * chunk, *slots[at % 2])
        if at > 0:
            add_up((at - 1) * chunk, *slots[(at - 1) % 2])


def kernel_body(own_points, far_points, *refs):
    groups = refs[:2]
    outs = refs[2:6]
    columns, rows = refs[6:]
    count, _, lanes = groups[0].shape
    size = count * lanes
    for which, messages in enumerate(groups):
        for at in range(count):
            uv = unpack(messages[at])[3:5]
            normal = jnp.sqrt(1.0 - uv[0:1] * uv[0:1] - uv[1:2] * uv[1:2])
            pad = jnp.zeros((5, lanes), F32)
            base = which * size + at * lanes
            columns[base : base + lanes, :] = jnp.concatenate([uv, normal, pad], axis=0).T
    for which, points in enumerate((own_points, far_points)):
        for at in range(2):
            base = (2 * which + at) * lanes
            for k, row in enumerate(point_rows(points, at)[:3]):
                rows[k : k + 1, base : base + lanes] = points[row : row + 1, :]
    for which in range(2):
        kernel_re, kernel_im = outs[2 * which : 2 * which + 2]

        def one(at, carry):
            start = pl.multiple_of(at * TILE, TILE)
            here = pl.ds(start, TILE)
            from_ = pl.ds(pl.multiple_of(which * size + start, TILE), TILE)
            turns = (
                columns[from_, 0:1] * rows[0:1, :]
                + columns[from_, 1:2] * rows[1:2, :]
                + columns[from_, 2:3] * rows[2:3, :]
            )
            cosine, sine = circle(turns, 1.0)
            kernel_re[here, :] = cosine.astype(BF16)
            kernel_im[here, :] = sine.astype(BF16)
            return carry

        lax.fori_loop(0, size // TILE, one, 0, unroll=16)


def radiate(kernel_re, kernel_im, held):
    return jnp.dot(kernel_re[...], held, preferred_element_type=F32) + jnp.dot(
        kernel_im[...], turned(held), preferred_element_type=F32
    )


def side_body(mine, theirs, kernel_re, kernel_im, currents, out):
    half = mine.shape[0] // 2
    for here, there in ((slice(0, half), slice(half, None)), (slice(half, None), slice(0, half))):
        currents[here, :] = (mine[here, :] + theirs[there, :].astype(F32)).astype(BF16)
    out[...] = radiate(kernel_re, kernel_im, currents[...]).astype(out.dtype)


def near_body(currents, kernel_re, kernel_im, out):
    out[...] = radiate(kernel_re, kernel_im, currents[...])


def fold_body(mine, theirs, *outs):
    total = mine[...] + theirs[...].astype(F32)
    start = 0
    for out in outs:
        out[...] = total[start : start + out.shape[0]].astype(out.dtype)
        start += out.shape[0]


def pass_body(*refs):
    total = refs[0][...].astype(F32)
    for ref in refs[1:-1]:
        total = total + ref[...].astype(F32)
    refs[-1][...] = total.astype(BF16)


def finish_body(kept, *refs):
    total = kept[...]
    rows = total.shape[0]
    for ref in refs[:-1]:
        total = total + ref[0:rows, :].astype(F32)
    refs[-1][...] = total


def call(body, outs, scratch=(), flops=0, anywhere=0, room=32 << 20):
    places = [pl.BlockSpec(memory_space=pltpu.HBM)] * anywhere
    return pl.pallas_call(
        body,
        out_shape=[jax.ShapeDtypeStruct(*out) for out in outs],
        scratch_shapes=list(scratch),
        compiler_params=pltpu.CompilerParams(vmem_limit_bytes=room),
        cost_estimate=pl.CostEstimate(flops=flops, bytes_accessed=0, transcendentals=0),
        **(dict(in_specs=places) if anywhere else {}),
    )


def per_device(
    feed_plane,
    feed_height,
    feed_weights,
    point_plane,
    point_height,
    patch_factor,
    direction_cosines,
):
    size = lax.axis_size("refl")
    line = size // 4
    sources, lanes = feed_weights.shape
    local_points = point_height.shape[0]
    half_points = 2 * local_points
    directions = direction_cosines.shape[1]

    def pairs(step):
        out = []
        for at in range(size):
            row, place = divmod(at, 4)
            far, near = divmod(step, 4)
            to = (row ^ far) if line & (line - 1) == 0 else (row + far) % line
            out.append((at, to * 4 + (place ^ near)))
        return out

    def swap(x, step, back=False, odd_step=None):
        links = pairs(step)
        if odd_step is not None:
            links = links[::2] + pairs(odd_step)[1::2]
        return lax.ppermute(x, "refl", [(b, a) for a, b in links] if back else links)

    message, points = call(
        pack_body,
        [((sources + PACK_ROWS, lanes), BF16), ((8, lanes), F32)],
        [pltpu.VMEM((8, lanes), F32), pltpu.VMEM((2, 2 * lanes), F32), pltpu.SemaphoreType.DMA((7,))],
        anywhere=7,
        room=32 << 20,
    )(
        *[
            pltpu.with_memory_space_constraint(x, pltpu.HBM)
            for x in (
                feed_weights,
                feed_plane,
                feed_height.reshape(1, lanes),
                direction_cosines,
                point_plane,
                point_height.reshape(2, lanes),
                patch_factor.reshape(2, lanes),
            )
        ]
    )
    arrived = [swap(message, 4 * k + 1) for k in range(1, line)]
    far_points = swap(points, 3)
    far_points, *arrived = lax.optimization_barrier((far_points, *arrived))
    near_messages = jnp.stack([message, *arrived])
    side_messages = swap(near_messages, 1)

    part = line * sources
    chunk = local_points
    scale = 1.0 / math.sqrt(local_points * size)

    def green(points, messages, bases, types):
        rows = len(points) * local_points
        slot = [((chunk, part), BF16), ((chunk, part), BF16), ((chunk, part), F32)]
        scratch = [
            ((rows, 4), F32),
            ((rows, TERMS), BF16),
            ((8, part), F32),
            ((TERMS, part), BF16),
            ((part, lanes), BF16),
            ((part, lanes), BF16),
            *slot,
            *slot,
        ]
        scratch = [pltpu.VMEM(*which) for which in scratch]
        return call(
            functools.partial(green_body, len(points), len(bases), scale),
            [((rows, lanes), kind) for kind in types],
            scratch,
            0,
        )(*points, messages, *bases)

    sets = [points, far_points]
    bases = green(sets, near_messages, [], [F32])
    mine, told = green(sets, side_messages, bases, [F32, BF16])
    theirs = swap(told, 3)

    even = lax.rem(lax.axis_index("refl"), 2) == 0
    near, side = ([x[k, sources:] for k in range(line)] for x in (near_messages, side_messages))
    keep, give = [near[0]], [side[0]]
    middle = [line // 2] if line % 2 == 0 and line > 1 else []
    for k in middle:
        keep.append(near[k])
        give.append(side[k])
    couples = [(k, line - k) for k in range(1, (line + 1) // 2)]
    for low, high in couples:
        keep += [jnp.where(even, side[low], side[high]), jnp.where(even, near[low], near[high])]
        give += [jnp.where(even, near[high], near[low]), jnp.where(even, side[high], side[low])]

    count = line * directions
    near_re, near_im, side_re, side_im = call(
        kernel_body,
        [((count, half_points), BF16)] * 4,
        [pltpu.VMEM((2 * count, 8), F32), pltpu.VMEM((8, half_points), F32)],
        60 * count * half_points,
    )(points, far_points, jnp.stack(keep), jnp.stack(give))
    currents, told = call(side_body, [((half_points, lanes), BF16), ((count, lanes), BF16)])(
        mine, theirs, side_re, side_im
    )
    given = swap(told, 1)
    near = call(near_body, [((count, lanes), F32)])(currents, near_re, near_im)[0]
    block, double = (directions, lanes), (2 * directions, lanes)
    kept, *sent = call(
        fold_body,
        [(block, F32)] + [(block, BF16)] * len(middle) + [(double, BF16)] * len(couples),
    )(near, given)
    doubles = [
        swap(x, 4 * low, back=True, odd_step=4 * high)
        for x, (low, high) in zip(sent[len(middle) :], couples)
    ]
    singles = [swap(x, 4 * k + 1, back=True) for x, k in zip(sent, middle)]
    arrived = singles + doubles
    if doubles:
        passed = [x[directions:] for x in doubles]
        if len(passed) > 1:
            passed = call(pass_body, [(block, BF16)])(*passed)
        arrived.append(swap(passed[0], 1))
    return call(finish_body, [((directions, lanes), F32)])(kept, *arrived)[0]


def solution(mesh):
    in_specs = (
        P("grp", "refl"),
        P(("grp", "refl")),
        P("refl", "grp"),
        P("grp", "refl"),
        P(("grp", "refl")),
        P(("grp", "refl")),
        P(None, "refl"),
    )
    out_specs = P("refl", "grp")
    return jax.shard_map(
        per_device, mesh=mesh, in_specs=in_specs, out_specs=out_specs, check_vma=False
    )
```

```python
import functools
import math

import jax
import jax.numpy as jnp
from jax import lax
from jax.experimental import pallas as pl
from jax.experimental.pallas import tpu as pltpu
from jax.sharding import PartitionSpec as P

RANGE_REF = 20.0
F32, BF16 = jnp.float32, jnp.bfloat16

SIN_HALF = (3.1415898893585, -5.167370491466989, 2.5435336188246254, -0.557959530770679)

ROUNDER = 1.5 * 2.0**23

TERMS = 32
MIDDLE = 22.0

COORDS = 5
PACK_ROWS = 16


def horner(square, terms, scale):
    total = jnp.float32(terms[-1] * scale)
    for term in terms[-2::-1]:
        total = total * square + jnp.float32(term * scale)
    return total


def half_turns(turns, flip):
    whole = (turns + ROUNDER) - ROUNDER
    part = whole - turns if flip else turns - whole
    sine = part * horner(part * part, SIN_HALF, math.sqrt(2.0))
    rest = jnp.maximum(2.0 - sine * sine, 1e-12)
    return sine, rest * lax.rsqrt(rest)


def turned(columns):
    half = columns.shape[1] // 2
    return jnp.concatenate([-columns[:, half:], columns[:, :half]], axis=1)


def pack_body(
    weights, feed_plane, feed_height, cosines, plane, height, patch, message, points, coords, ends, sems
):
    rows, lanes = weights.shape
    sources = [feed_plane, feed_height, cosines, plane, height, patch, weights]
    targets = [
        coords.at[0:2, :],
        coords.at[2:3, :],
        coords.at[3:5, :],
        ends,
        points.at[4:6, :],
        points.at[6:8, :],
        message.at[0:rows, :],
    ]
    copies = [
        pltpu.make_async_copy(source, target, sems.at[at])
        for at, (source, target) in enumerate(zip(sources, targets))
    ]
    for copy in copies[::-1]:
        copy.start()
    for copy in copies[:4]:
        copy.wait()
    points[0:2, :] = ends[:, :lanes]
    points[2:4, :] = ends[:, lanes:]
    exact = coords[0:COORDS, :]
    high = exact.astype(BF16)
    rest = exact - high.astype(F32)
    middle = rest.astype(BF16)
    low = (rest - middle.astype(F32)).astype(BF16)
    pad = jnp.zeros((PACK_ROWS - 3 * COORDS, lanes), F32)
    message[rows:, :] = jnp.concatenate(
        [high.astype(F32), middle.astype(F32), low.astype(F32), pad], axis=0
    ).astype(BF16)
    for copy in copies[4:]:
        copy.wait()


def unpack(tail):
    tail = tail.astype(F32)
    return (tail[:COORDS] + tail[COORDS : 2 * COORDS]) + tail[2 * COORDS : 3 * COORDS]


def split(value):
    high = value.astype(BF16).astype(F32)
    rest = value - high
    middle = rest.astype(BF16).astype(F32)
    return high, middle, (rest - middle).astype(BF16).astype(F32)


def distance_terms(x, y, z, is_point):
    z = z - MIDDLE
    square = x * x + y * y + z * z
    out = []
    for value in (x, y, z):
        high, middle, low = split(value if is_point else -2.0 * value)
        out += [high, high, middle, high, middle, low] if is_point else [high, middle, high, low, middle, high]
    ones = [jnp.ones_like(x)] * 3
    out += list(split(square)) + ones if is_point else ones + list(split(square))
    return jnp.concatenate(out + [jnp.zeros_like(x)] * (TERMS - len(out)), axis=0)


def point_rows(points, at):
    return (2 * at, 2 * at + 1, 4 + at, 6 + at)


def fill_point_columns(points, columns, base):
    lanes = points.shape[1]
    up = points[...].T
    for at in range(2):
        columns[base + at * lanes : base + (at + 1) * lanes, :] = jnp.concatenate(
            [up[:, k : k + 1] for k in point_rows(points, at)], axis=1
        )


TILE = 32
LANES = 512


def blocks(total, most):
    return [slice(at, min(at + most, total)) for at in range(0, total, most)]


def green_body(point_sets, bases, scale, *refs):
    points, messages, refs = refs[:point_sets], refs[point_sets], refs[point_sets + 1 :]
    base, outs = refs[:bases], refs[bases:-12]
    columns, left, heights, right, weights, weights_turned, *slots = refs[-12:]
    slots = (slots[:3], slots[3:])
    count, height, lanes = messages.shape
    sources = height - PACK_ROWS
    total_points = columns.shape[0]
    for at in range(point_sets):
        fill_point_columns(points[at], columns, 2 * lanes * at)
        for half in range(2):
            x, y, z = (points[at][k : k + 1, :] for k in point_rows(points[at], half)[:3])
            start = (2 * at + half) * lanes
            left[start : start + lanes, :] = distance_terms(x, y, z, True).T.astype(BF16)
    for at in range(count):
        where = slice(at * sources, (at + 1) * sources)
        coords = unpack(messages[at, sources:, :])
        x, y, z = coords[0:1], coords[1:2], coords[2:3]
        heights[0:1, where] = z * RANGE_REF
        right[:, where] = distance_terms(x, y, z, False).astype(BF16)
        block = messages[at, :sources, :]
        weights[where, :] = block
        weights_turned[where, :] = turned(block)
    chunk = slots[0][0].shape[0]

    def fill(start, green_re, green_im, squares):
        squares[...] = jnp.dot(
            left[start : start + chunk, :], right[...], preferred_element_type=F32
        )
        for at in range(0, chunk, TILE):
            low = columns[start + at : start + at + TILE, 2:3] * RANGE_REF
            for part in blocks(count * sources, LANES):
                squared = squares[at : at + TILE, part]
                inverse = lax.rsqrt(squared)
                sine, cosine = half_turns(squared * inverse, True)
                amplitude = (heights[0:1, part] - low) * (inverse * inverse)
                scaled = amplitude * sine
                green_re[at : at + TILE, part] = (amplitude - scaled * sine).astype(BF16)
                green_im[at : at + TILE, part] = (scaled * cosine).astype(BF16)

    def add_up(start, green_re, green_im, _):
        here = slice(start, start + chunk)
        total = jnp.dot(green_re[...], weights[...], preferred_element_type=F32) + jnp.dot(
            green_im[...], weights_turned[...], preferred_element_type=F32
        )
        if base:
            step = base[0].shape[0]
            held = base[start // step][start % step : start % step + chunk, :]
            total = (total + held) * (columns[here, 3:4] * scale)
        for out in outs:
            out[here, :] = total.astype(out.dtype)

    turns = total_points // chunk
    for at in range(turns + 1):
        if at < turns:
            fill(at * chunk, *slots[at % 2])
        if at > 0:
            add_up((at - 1) * chunk, *slots[(at - 1) % 2])


def kernel_body(own_points, far_points, *refs):
    groups = refs[:2]
    outs = refs[2:6]
    columns, rows = refs[6:]
    count, _, lanes = groups[0].shape
    size = count * lanes
    for which, messages in enumerate(groups):
        for at in range(count):
            uv = unpack(messages[at])[3:5]
            normal = jnp.sqrt(1.0 - uv[0:1] * uv[0:1] - uv[1:2] * uv[1:2])
            pad = jnp.zeros((5, lanes), F32)
            base = which * size + at * lanes
            columns[base : base + lanes, :] = jnp.concatenate([uv, normal, pad], axis=0).T
    for which, points in enumerate((own_points, far_points)):
        for at in range(2):
            base = (2 * which + at) * lanes
            for k, row in enumerate(point_rows(points, at)[:3]):
                rows[k : k + 1, base : base + lanes] = points[row : row + 1, :]
    for which in range(2):
        kernel_re, kernel_im = outs[2 * which : 2 * which + 2]

        def one(at, carry):
            start = pl.multiple_of(at * TILE, TILE)
            here = pl.ds(start, TILE)
            from_ = pl.ds(pl.multiple_of(which * size + start, TILE), TILE)
            turns = (
                columns[from_, 0:1] * rows[0:1, :]
                + columns[from_, 1:2] * rows[1:2, :]
                + columns[from_, 2:3] * rows[2:3, :]
            )
            sine, cosine = half_turns(turns, False)
            kernel_re[here, :] = (1.0 - sine * sine).astype(BF16)
            kernel_im[here, :] = (sine * cosine).astype(BF16)
            return carry

        lax.fori_loop(0, size // TILE, one, 0, unroll=16)


def radiate(kernel_re, kernel_im, held):
    return jnp.dot(kernel_re[...], held, preferred_element_type=F32) + jnp.dot(
        kernel_im[...], turned(held), preferred_element_type=F32
    )


def side_body(mine, theirs, kernel_re, kernel_im, currents, out):
    half = mine.shape[0] // 2
    for here, there in ((slice(0, half), slice(half, None)), (slice(half, None), slice(0, half))):
        currents[here, :] = (mine[here, :] + theirs[there, :].astype(F32)).astype(BF16)
    out[...] = radiate(kernel_re, kernel_im, currents[...]).astype(out.dtype)


def near_body(currents, kernel_re, kernel_im, out):
    out[...] = radiate(kernel_re, kernel_im, currents[...])


def fold_body(mine, theirs, *outs):
    total = mine[...] + theirs[...].astype(F32)
    start = 0
    for out in outs:
        out[...] = total[start : start + out.shape[0]].astype(out.dtype)
        start += out.shape[0]


def pass_body(*refs):
    total = refs[0][...].astype(F32)
    for ref in refs[1:-1]:
        total = total + ref[...].astype(F32)
    refs[-1][...] = total.astype(BF16)


def finish_body(kept, *refs):
    total = kept[...]
    rows = total.shape[0]
    for ref in refs[:-1]:
        total = total + ref[0:rows, :].astype(F32)
    refs[-1][...] = total


def call(body, outs, scratch=(), flops=0, anywhere=0, room=32 << 20):
    places = [pl.BlockSpec(memory_space=pltpu.HBM)] * anywhere
    return pl.pallas_call(
        body,
        out_shape=[jax.ShapeDtypeStruct(*out) for out in outs],
        scratch_shapes=list(scratch),
        compiler_params=pltpu.CompilerParams(vmem_limit_bytes=room),
        cost_estimate=pl.CostEstimate(flops=flops, bytes_accessed=0, transcendentals=0),
        **(dict(in_specs=places) if anywhere else {}),
    )


def per_device(
    feed_plane,
    feed_height,
    feed_weights,
    point_plane,
    point_height,
    patch_factor,
    direction_cosines,
):
    size = lax.axis_size("refl")
    line = size // 4
    sources, lanes = feed_weights.shape
    local_points = point_height.shape[0]
    half_points = 2 * local_points
    directions = direction_cosines.shape[1]

    def pairs(step):
        out = []
        for at in range(size):
            row, place = divmod(at, 4)
            far, near = divmod(step, 4)
            to = (row ^ far) if line & (line - 1) == 0 else (row + far) % line
            out.append((at, to * 4 + (place ^ near)))
        return out

    def swap(x, step, back=False, odd_step=None):
        links = pairs(step)
        if odd_step is not None:
            links = links[::2] + pairs(odd_step)[1::2]
        return lax.ppermute(x, "refl", [(b, a) for a, b in links] if back else links)

    message, points = call(
        pack_body,
        [((sources + PACK_ROWS, lanes), BF16), ((8, lanes), F32)],
        [pltpu.VMEM((8, lanes), F32), pltpu.VMEM((2, 2 * lanes), F32), pltpu.SemaphoreType.DMA((7,))],
        anywhere=7,
        room=32 << 20,
    )(
        *[
            pltpu.with_memory_space_constraint(x, pltpu.HBM)
            for x in (
                feed_weights,
                feed_plane,
                feed_height.reshape(1, lanes),
                direction_cosines,
                point_plane,
                point_height.reshape(2, lanes),
                patch_factor.reshape(2, lanes),
            )
        ]
    )
    arrived = [swap(message, 4 * k + 1) for k in range(1, line)]
    far_points = swap(points, 3)
    far_points, *arrived = lax.optimization_barrier((far_points, *arrived))
    near_messages = jnp.stack([message, *arrived])
    side_messages = swap(near_messages, 1)

    part = line * sources
    chunk = local_points
    scale = 1.0 / math.sqrt(local_points * size)

    def green(points, messages, bases, types):
        rows = len(points) * local_points
        slot = [((chunk, part), BF16), ((chunk, part), BF16), ((chunk, part), F32)]
        scratch = [
            ((rows, 4), F32),
            ((rows, TERMS), BF16),
            ((8, part), F32),
            ((TERMS, part), BF16),
            ((part, lanes), BF16),
            ((part, lanes), BF16),
            *slot,
            *slot,
        ]
        scratch = [pltpu.VMEM(*which) for which in scratch]
        return call(
            functools.partial(green_body, len(points), len(bases), scale),
            [((rows, lanes), kind) for kind in types],
            scratch,
            0,
        )(*points, messages, *bases)

    sets = [points, far_points]
    bases = green(sets, near_messages, [], [F32])
    mine, told = green(sets, side_messages, bases, [F32, BF16])
    theirs = swap(told, 3)

    even = lax.rem(lax.axis_index("refl"), 2) == 0
    near, side = ([x[k, sources:] for k in range(line)] for x in (near_messages, side_messages))
    keep, give = [near[0]], [side[0]]
    middle = [line // 2] if line % 2 == 0 and line > 1 else []
    for k in middle:
        keep.append(near[k])
        give.append(side[k])
    couples = [(k, line - k) for k in range(1, (line + 1) // 2)]
    for low, high in couples:
        keep += [jnp.where(even, side[low], side[high]), jnp.where(even, near[low], near[high])]
        give += [jnp.where(even, near[high], near[low]), jnp.where(even, side[high], side[low])]

    count = line * directions
    near_re, near_im, side_re, side_im = call(
        kernel_body,
        [((count, half_points), BF16)] * 4,
        [pltpu.VMEM((2 * count, 8), F32), pltpu.VMEM((8, half_points), F32)],
        60 * count * half_points,
    )(points, far_points, jnp.stack(keep), jnp.stack(give))
    currents, told = call(side_body, [((half_points, lanes), BF16), ((count, lanes), BF16)])(
        mine, theirs, side_re, side_im
    )
    given = swap(told, 1)
    near = call(near_body, [((count, lanes), F32)])(currents, near_re, near_im)[0]
    block, double = (directions, lanes), (2 * directions, lanes)
    kept, *sent = call(
        fold_body,
        [(block, F32)] + [(block, BF16)] * len(middle) + [(double, BF16)] * len(couples),
    )(near, given)
    doubles = [
        swap(x, 4 * low, back=True, odd_step=4 * high)
        for x, (low, high) in zip(sent[len(middle) :], couples)
    ]
    singles = [swap(x, 4 * k + 1, back=True) for x, k in zip(sent, middle)]
    arrived = singles + doubles
    if doubles:
        passed = [x[directions:] for x in doubles]
        if len(passed) > 1:
            passed = call(pass_body, [(block, BF16)])(*passed)
        arrived.append(swap(passed[0], 1))
    return call(finish_body, [((directions, lanes), F32)])(kept, *arrived)[0]


def solution(mesh):
    in_specs = (
        P("grp", "refl"),
        P(("grp", "refl")),
        P("refl", "grp"),
        P("grp", "refl"),
        P(("grp", "refl")),
        P(("grp", "refl")),
        P(None, "refl"),
    )
    out_specs = P("refl", "grp")
    return jax.shard_map(
        per_device, mesh=mesh, in_specs=in_specs, out_specs=out_specs, check_vma=False
    )
```

```python
import functools
import math

import jax
import jax.numpy as jnp
from jax import lax
from jax.experimental import pallas as pl
from jax.experimental.pallas import tpu as pltpu
from jax.sharding import PartitionSpec as P

RANGE_REF = 20.0
F32, BF16 = jnp.float32, jnp.bfloat16

SIN_HALF = (3.1415898893585, -5.167370491466989, 2.5435336188246254, -0.557959530770679)

ROUNDER = 1.5 * 2.0**23

TERMS = 32
MIDDLE = 22.0

COORDS = 5
PACK_ROWS = 16


def horner(square, terms, scale):
    total = jnp.float32(terms[-1] * scale)
    for term in terms[-2::-1]:
        total = total * square + jnp.float32(term * scale)
    return total


def half_turns(turns, flip):
    whole = (turns + ROUNDER) - ROUNDER
    part = whole - turns if flip else turns - whole
    sine = part * horner(part * part, SIN_HALF, math.sqrt(2.0))
    rest = jnp.maximum(2.0 - sine * sine, 1e-12)
    return sine, rest * lax.rsqrt(rest)


def turned(columns):
    half = columns.shape[1] // 2
    return jnp.concatenate([-columns[:, half:], columns[:, :half]], axis=1)


def pack_body(
    weights, feed_plane, feed_height, cosines, plane, height, patch, message, points, coords, ends, sems
):
    rows, lanes = weights.shape
    sources = [feed_plane, feed_height, cosines, plane, height, patch, weights]
    targets = [
        coords.at[0:2, :],
        coords.at[2:3, :],
        coords.at[3:5, :],
        ends,
        points.at[4:6, :],
        points.at[6:8, :],
        message.at[0:rows, :],
    ]
    copies = [
        pltpu.make_async_copy(source, target, sems.at[at])
        for at, (source, target) in enumerate(zip(sources, targets))
    ]
    for copy in copies[::-1]:
        copy.start()
    for copy in copies[:4]:
        copy.wait()
    points[0:2, :] = ends[:, :lanes]
    points[2:4, :] = ends[:, lanes:]
    exact = coords[0:COORDS, :]
    high = exact.astype(BF16)
    rest = exact - high.astype(F32)
    middle = rest.astype(BF16)
    low = (rest - middle.astype(F32)).astype(BF16)
    pad = jnp.zeros((PACK_ROWS - 3 * COORDS, lanes), F32)
    message[rows:, :] = jnp.concatenate(
        [high.astype(F32), middle.astype(F32), low.astype(F32), pad], axis=0
    ).astype(BF16)
    for copy in copies[4:]:
        copy.wait()


def unpack(tail):
    tail = tail.astype(F32)
    return (tail[:COORDS] + tail[COORDS : 2 * COORDS]) + tail[2 * COORDS : 3 * COORDS]


def split(value):
    high = value.astype(BF16).astype(F32)
    rest = value - high
    middle = rest.astype(BF16).astype(F32)
    return high, middle, (rest - middle).astype(BF16).astype(F32)


def distance_terms(x, y, z, is_point):
    z = z - MIDDLE
    square = x * x + y * y + z * z
    out = []
    for value in (x, y, z):
        high, middle, low = split(value if is_point else -2.0 * value)
        out += [high, high, middle, high, middle, low] if is_point else [high, middle, high, low, middle, high]
    ones = [jnp.ones_like(x)] * 3
    out += list(split(square)) + ones if is_point else ones + list(split(square))
    return jnp.concatenate(out + [jnp.zeros_like(x)] * (TERMS - len(out)), axis=0)


def point_rows(points, at):
    return (2 * at, 2 * at + 1, 4 + at, 6 + at)


def fill_point_columns(points, columns, base):
    lanes = points.shape[1]
    up = points[...].T
    for at in range(2):
        columns[base + at * lanes : base + (at + 1) * lanes, :] = jnp.concatenate(
            [up[:, k : k + 1] for k in point_rows(points, at)], axis=1
        )


TILE = 32
LANES = 512


def blocks(total, most):
    return [slice(at, min(at + most, total)) for at in range(0, total, most)]


def green_body(point_sets, bases, scale, *refs):
    points, messages, refs = refs[:point_sets], refs[point_sets], refs[point_sets + 1 :]
    if bases:
        base, (columns, left), outs = refs[:bases], refs[bases : bases + 2], refs[bases + 2 : -10]
    else:
        base, outs, (columns, left) = (), refs[:-12], refs[-12:-10]
    heights, right, weights, weights_turned, *slots = refs[-10:]
    slots = (slots[:3], slots[3:])
    count, height, lanes = messages.shape
    sources = height - PACK_ROWS
    total_points = columns.shape[0]
    for at in range(0 if bases else point_sets):
        fill_point_columns(points[at], columns, 2 * lanes * at)
        for half in range(2):
            x, y, z = (points[at][k : k + 1, :] for k in point_rows(points[at], half)[:3])
            start = (2 * at + half) * lanes
            left[start : start + lanes, :] = distance_terms(x, y, z, True).T.astype(BF16)
    for at in range(count):
        where = slice(at * sources, (at + 1) * sources)
        coords = unpack(messages[at, sources:, :])
        x, y, z = coords[0:1], coords[1:2], coords[2:3]
        heights[0:1, where] = z * RANGE_REF
        right[:, where] = distance_terms(x, y, z, False).astype(BF16)
        block = messages[at, :sources, :]
        weights[where, :] = block
        weights_turned[where, :] = turned(block)
    chunk = slots[0][0].shape[0]

    def fill(start, green_re, green_im, squares):
        squares[...] = jnp.dot(
            left[start : start + chunk, :], right[...], preferred_element_type=F32
        )
        for at in range(0, chunk, TILE):
            low = columns[start + at : start + at + TILE, 2:3] * RANGE_REF
            for part in blocks(count * sources, LANES):
                squared = squares[at : at + TILE, part]
                inverse = lax.rsqrt(squared)
                sine, cosine = half_turns(squared * inverse, True)
                amplitude = (heights[0:1, part] - low) * (inverse * inverse)
                scaled = amplitude * sine
                green_re[at : at + TILE, part] = (amplitude - scaled * sine).astype(BF16)
                green_im[at : at + TILE, part] = (scaled * cosine).astype(BF16)

    def add_up(start, green_re, green_im, _):
        here = slice(start, start + chunk)
        total = jnp.dot(green_re[...], weights[...], preferred_element_type=F32) + jnp.dot(
            green_im[...], weights_turned[...], preferred_element_type=F32
        )
        if base:
            step = base[0].shape[0]
            held = base[start // step][start % step : start % step + chunk, :]
            total = (total + held) * (columns[here, 3:4] * scale)
        for out in outs:
            out[here, :] = total.astype(out.dtype)

    turns = total_points // chunk
    for at in range(turns + 1):
        if at < turns:
            fill(at * chunk, *slots[at % 2])
        if at > 0:
            add_up((at - 1) * chunk, *slots[(at - 1) % 2])


def kernel_body(own_points, far_points, *refs):
    groups = refs[:2]
    outs = refs[2:6]
    columns, rows = refs[6:]
    count, _, lanes = groups[0].shape
    size = count * lanes
    for which, messages in enumerate(groups):
        for at in range(count):
            uv = unpack(messages[at])[3:5]
            normal = jnp.sqrt(1.0 - uv[0:1] * uv[0:1] - uv[1:2] * uv[1:2])
            pad = jnp.zeros((5, lanes), F32)
            base = which * size + at * lanes
            columns[base : base + lanes, :] = jnp.concatenate([uv, normal, pad], axis=0).T
    for which, points in enumerate((own_points, far_points)):
        for at in range(2):
            base = (2 * which + at) * lanes
            for k, row in enumerate(point_rows(points, at)[:3]):
                rows[k : k + 1, base : base + lanes] = points[row : row + 1, :]
    for which in range(2):
        kernel_re, kernel_im = outs[2 * which : 2 * which + 2]

        def one(at, carry):
            start = pl.multiple_of(at * TILE, TILE)
            here = pl.ds(start, TILE)
            from_ = pl.ds(pl.multiple_of(which * size + start, TILE), TILE)
            turns = (
                columns[from_, 0:1] * rows[0:1, :]
                + columns[from_, 1:2] * rows[1:2, :]
                + columns[from_, 2:3] * rows[2:3, :]
            )
            sine, cosine = half_turns(turns, False)
            kernel_re[here, :] = (1.0 - sine * sine).astype(BF16)
            kernel_im[here, :] = (sine * cosine).astype(BF16)
            return carry

        lax.fori_loop(0, size // TILE, one, 0, unroll=16)


def radiate(kernel_re, kernel_im, held, held_turned):
    return jnp.dot(kernel_re[...], held[...], preferred_element_type=F32) + jnp.dot(
        kernel_im[...], held_turned[...], preferred_element_type=F32
    )


def side_body(mine, theirs, kernel_re, kernel_im, held, held_turned, out):
    half, lanes = mine.shape[0] // 2, mine.shape[1]
    is_real = lax.broadcasted_iota(jnp.int32, (half, lanes), 1) < lanes // 2
    for here, there in ((slice(0, half), slice(half, None)), (slice(half, None), slice(0, half))):
        total = mine[here, :] + theirs[there, :].astype(F32)
        moved = pltpu.roll(total, lanes // 2, 1)
        held[here, :] = total.astype(BF16)
        held_turned[here, :] = jnp.where(is_real, -moved, moved).astype(BF16)
    out[...] = radiate(kernel_re, kernel_im, held, held_turned).astype(out.dtype)


def near_body(held, held_turned, kernel_re, kernel_im, out):
    out[...] = radiate(kernel_re, kernel_im, held, held_turned)


def fold_body(mine, theirs, *outs):
    total = mine[...] + theirs[...].astype(F32)
    start = 0
    for out in outs:
        out[...] = total[start : start + out.shape[0]].astype(out.dtype)
        start += out.shape[0]


def pass_body(*refs):
    total = refs[0][...].astype(F32)
    for ref in refs[1:-1]:
        total = total + ref[...].astype(F32)
    refs[-1][...] = total.astype(BF16)


def finish_body(kept, *refs):
    total = kept[...]
    rows = total.shape[0]
    for ref in refs[:-1]:
        total = total + ref[0:rows, :].astype(F32)
    refs[-1][...] = total


def call(body, outs, scratch=(), flops=0, anywhere=0, room=32 << 20):
    places = [pl.BlockSpec(memory_space=pltpu.HBM)] * anywhere
    return pl.pallas_call(
        body,
        out_shape=[jax.ShapeDtypeStruct(*out) for out in outs],
        scratch_shapes=list(scratch),
        compiler_params=pltpu.CompilerParams(vmem_limit_bytes=room),
        cost_estimate=pl.CostEstimate(flops=flops, bytes_accessed=0, transcendentals=0),
        **(dict(in_specs=places) if anywhere else {}),
    )


def per_device(
    feed_plane,
    feed_height,
    feed_weights,
    point_plane,
    point_height,
    patch_factor,
    direction_cosines,
):
    size = lax.axis_size("refl")
    line = size // 4
    sources, lanes = feed_weights.shape
    local_points = point_height.shape[0]
    half_points = 2 * local_points
    directions = direction_cosines.shape[1]

    def pairs(step):
        out = []
        for at in range(size):
            row, place = divmod(at, 4)
            far, near = divmod(step, 4)
            to = (row ^ far) if line & (line - 1) == 0 else (row + far) % line
            out.append((at, to * 4 + (place ^ near)))
        return out

    def swap(x, step, back=False, odd_step=None):
        links = pairs(step)
        if odd_step is not None:
            links = links[::2] + pairs(odd_step)[1::2]
        return lax.ppermute(x, "refl", [(b, a) for a, b in links] if back else links)

    message, points = call(
        pack_body,
        [((sources + PACK_ROWS, lanes), BF16), ((8, lanes), F32)],
        [pltpu.VMEM((8, lanes), F32), pltpu.VMEM((2, 2 * lanes), F32), pltpu.SemaphoreType.DMA((7,))],
        anywhere=7,
        room=32 << 20,
    )(
        *[
            pltpu.with_memory_space_constraint(x, pltpu.HBM)
            for x in (
                feed_weights,
                feed_plane,
                feed_height.reshape(1, lanes),
                direction_cosines,
                point_plane,
                point_height.reshape(2, lanes),
                patch_factor.reshape(2, lanes),
            )
        ]
    )
    arrived = [swap(message, 4 * k + 1) for k in range(1, line)]
    far_points = swap(points, 3)
    far_points, *arrived = lax.optimization_barrier((far_points, *arrived))
    near_messages = jnp.stack([message, *arrived])
    side_messages = swap(near_messages, 1)

    part = line * sources
    chunk = local_points
    scale = 1.0 / math.sqrt(local_points * size)

    def green(points, messages, bases, types):
        rows = len(points) * local_points
        slot = [((chunk, part), BF16), ((chunk, part), BF16), ((chunk, part), F32)]
        tables = [] if bases else [((rows, 4), F32), ((rows, TERMS), BF16)]
        scratch = [
            ((8, part), F32),
            ((TERMS, part), BF16),
            ((part, lanes), BF16),
            ((part, lanes), BF16),
            *slot,
            *slot,
        ]
        scratch = [pltpu.VMEM(*which) for which in scratch]
        return call(
            functools.partial(green_body, len(points), len(bases[:1]), scale),
            [((rows, lanes), kind) for kind in types] + tables,
            scratch,
            0,
        )(*points, messages, *bases)

    sets = [points, far_points]
    first, *tables = green(sets, near_messages, [], [F32])
    mine, told = green(sets, side_messages, [first, *tables], [F32, BF16])
    theirs = swap(told, 3)

    even = lax.rem(lax.axis_index("refl"), 2) == 0
    near, side = ([x[k, sources:] for k in range(line)] for x in (near_messages, side_messages))
    keep, give = [near[0]], [side[0]]
    middle = [line // 2] if line % 2 == 0 and line > 1 else []
    for k in middle:
        keep.append(near[k])
        give.append(side[k])
    couples = [(k, line - k) for k in range(1, (line + 1) // 2)]
    for low, high in couples:
        keep += [jnp.where(even, side[low], side[high]), jnp.where(even, near[low], near[high])]
        give += [jnp.where(even, near[high], near[low]), jnp.where(even, side[high], side[low])]

    count = line * directions
    near_re, near_im, side_re, side_im = call(
        kernel_body,
        [((count, half_points), BF16)] * 4,
        [pltpu.VMEM((2 * count, 8), F32), pltpu.VMEM((8, half_points), F32)],
        60 * count * half_points,
    )(points, far_points, jnp.stack(keep), jnp.stack(give))
    *currents, told = call(
        side_body, [((half_points, lanes), BF16)] * 2 + [((count, lanes), BF16)]
    )(mine, theirs, side_re, side_im)
    given = swap(told, 1)
    near = call(near_body, [((count, lanes), F32)])(*currents, near_re, near_im)[0]
    block, double = (directions, lanes), (2 * directions, lanes)
    kept, *sent = call(
        fold_body,
        [(block, F32)] + [(block, BF16)] * len(middle) + [(double, BF16)] * len(couples),
    )(near, given)
    doubles = [
        swap(x, 4 * low, back=True, odd_step=4 * high)
        for x, (low, high) in zip(sent[len(middle) :], couples)
    ]
    singles = [swap(x, 4 * k + 1, back=True) for x, k in zip(sent, middle)]
    arrived = singles + doubles
    if doubles:
        passed = [x[directions:] for x in doubles]
        if len(passed) > 1:
            passed = call(pass_body, [(block, BF16)])(*passed)
        arrived.append(swap(passed[0], 1))
    return call(finish_body, [((directions, lanes), F32)])(kept, *arrived)[0]


def solution(mesh):
    in_specs = (
        P("grp", "refl"),
        P(("grp", "refl")),
        P("refl", "grp"),
        P("grp", "refl"),
        P(("grp", "refl")),
        P(("grp", "refl")),
        P(None, "refl"),
    )
    out_specs = P("refl", "grp")
    return jax.shard_map(
        per_device, mesh=mesh, in_specs=in_specs, out_specs=out_specs, check_vma=False
    )
```

```python
import functools
import math

import jax
import jax.numpy as jnp
from jax import lax
from jax.experimental import pallas as pl
from jax.experimental.pallas import tpu as pltpu
from jax.sharding import PartitionSpec as P

RANGE_REF = 20.0
F32, BF16 = jnp.float32, jnp.bfloat16

SIN_HALF = (3.1415898893585, -5.167370491466989, 2.5435336188246254, -0.557959530770679)

ROUNDER = 1.5 * 2.0**23

TERMS = 32
MIDDLE = 22.0

COORDS = 5
PACK_ROWS = 16


def horner(square, terms, scale):
    total = jnp.float32(terms[-1] * scale)
    for term in terms[-2::-1]:
        total = total * square + jnp.float32(term * scale)
    return total


def half_turns(turns, flip):
    whole = (turns + ROUNDER) - ROUNDER
    part = whole - turns if flip else turns - whole
    sine = part * horner(part * part, SIN_HALF, math.sqrt(2.0))
    rest = jnp.maximum(2.0 - sine * sine, 1e-12)
    return sine, rest * lax.rsqrt(rest)


def turned(columns):
    half = columns.shape[1] // 2
    return jnp.concatenate([-columns[:, half:], columns[:, :half]], axis=1)


def pack_body(
    weights, feed_plane, feed_height, cosines, plane, height, patch, message, points, coords, ends, sems
):
    rows, lanes = weights.shape
    sources = [feed_plane, feed_height, cosines, plane, height, patch, weights]
    targets = [
        coords.at[0:2, :],
        coords.at[2:3, :],
        coords.at[3:5, :],
        ends,
        points.at[4:6, :],
        points.at[6:8, :],
        message.at[0:rows, :],
    ]
    copies = [
        pltpu.make_async_copy(source, target, sems.at[at])
        for at, (source, target) in enumerate(zip(sources, targets))
    ]
    for copy in copies[::-1]:
        copy.start()
    for copy in copies[:4]:
        copy.wait()
    points[0:2, :] = ends[:, :lanes]
    points[2:4, :] = ends[:, lanes:]
    exact = coords[0:COORDS, :]
    high = exact.astype(BF16)
    rest = exact - high.astype(F32)
    middle = rest.astype(BF16)
    low = (rest - middle.astype(F32)).astype(BF16)
    pad = jnp.zeros((PACK_ROWS - 3 * COORDS, lanes), F32)
    message[rows:, :] = jnp.concatenate(
        [high.astype(F32), middle.astype(F32), low.astype(F32), pad], axis=0
    ).astype(BF16)
    for copy in copies[4:]:
        copy.wait()


def unpack(tail):
    tail = tail.astype(F32)
    return (tail[:COORDS] + tail[COORDS : 2 * COORDS]) + tail[2 * COORDS : 3 * COORDS]


def split(value):
    high = value.astype(BF16).astype(F32)
    rest = value - high
    middle = rest.astype(BF16).astype(F32)
    return high, middle, (rest - middle).astype(BF16).astype(F32)


def distance_terms(x, y, z, is_point):
    z = z - MIDDLE
    square = x * x + y * y + z * z
    out = []
    for value in (x, y, z):
        high, middle, low = split(value if is_point else -2.0 * value)
        out += [high, high, middle, high, middle, low] if is_point else [high, middle, high, low, middle, high]
    ones = [jnp.ones_like(x)] * 3
    out += list(split(square)) + ones if is_point else ones + list(split(square))
    return jnp.concatenate(out + [jnp.zeros_like(x)] * (TERMS - len(out)), axis=0)


def point_rows(points, at):
    return (2 * at, 2 * at + 1, 4 + at, 6 + at)


def fill_point_columns(points, columns, base):
    lanes = points.shape[1]
    up = points[...].T
    for at in range(2):
        columns[base + at * lanes : base + (at + 1) * lanes, :] = jnp.concatenate(
            [up[:, k : k + 1] for k in point_rows(points, at)], axis=1
        )


TILE = 32
LANES = 512


def blocks(total, most):
    return [slice(at, min(at + most, total)) for at in range(0, total, most)]


def green_body(point_sets, bases, scale, *refs):
    points, messages, refs = refs[:point_sets], refs[point_sets], refs[point_sets + 1 :]
    if bases:
        base, (columns, left), outs = refs[:bases], refs[bases : bases + 2], refs[bases + 2 : -10]
    else:
        base, outs, (columns, left) = (), refs[:-12], refs[-12:-10]
    heights, right, weights, weights_turned, *slots = refs[-10:]
    slots = (slots[:3], slots[3:])
    count, height, lanes = messages.shape
    sources = height - PACK_ROWS
    total_points = columns.shape[0]
    for at in range(0 if bases else point_sets):
        fill_point_columns(points[at], columns, 2 * lanes * at)
        for half in range(2):
            x, y, z = (points[at][k : k + 1, :] for k in point_rows(points[at], half)[:3])
            start = (2 * at + half) * lanes
            left[start : start + lanes, :] = distance_terms(x, y, z, True).T.astype(BF16)
    for at in range(count):
        where = slice(at * sources, (at + 1) * sources)
        coords = unpack(messages[at, sources:, :])
        x, y, z = coords[0:1], coords[1:2], coords[2:3]
        heights[0:1, where] = z * RANGE_REF
        right[:, where] = distance_terms(x, y, z, False).astype(BF16)
        block = messages[at, :sources, :]
        weights[where, :] = block
        weights_turned[where, :] = turned(block)
    chunk = slots[0][0].shape[0]

    def fill(start, green_re, green_im, squares):
        squares[...] = jnp.dot(
            left[start : start + chunk, :], right[...], preferred_element_type=F32
        )
        for at in range(0, chunk, TILE):
            low = columns[start + at : start + at + TILE, 2:3] * RANGE_REF
            for part in blocks(count * sources, LANES):
                squared = squares[at : at + TILE, part]
                inverse = lax.rsqrt(squared)
                sine, cosine = half_turns(squared * inverse, True)
                amplitude = (heights[0:1, part] - low) * (inverse * inverse)
                scaled = amplitude * sine
                green_re[at : at + TILE, part] = (amplitude - scaled * sine).astype(BF16)
                green_im[at : at + TILE, part] = (scaled * cosine).astype(BF16)

    def add_up(start, green_re, green_im, _):
        here = slice(start, start + chunk)
        total = jnp.dot(green_re[...], weights[...], preferred_element_type=F32) + jnp.dot(
            green_im[...], weights_turned[...], preferred_element_type=F32
        )
        if base:
            step = base[0].shape[0]
            held = base[start // step][start % step : start % step + chunk, :]
            total = (total + held) * (columns[here, 3:4] * scale)
        for out in outs:
            out[here, :] = total.astype(out.dtype)

    turns = total_points // chunk
    for at in range(turns + 1):
        if at < turns:
            fill(at * chunk, *slots[at % 2])
        if at > 0:
            add_up((at - 1) * chunk, *slots[(at - 1) % 2])


def kernel_body(own_points, far_points, *refs):
    groups = refs[:2]
    outs = refs[2:6]
    columns, rows = refs[6:]
    count, _, lanes = groups[0].shape
    size = count * lanes
    for which, messages in enumerate(groups):
        for at in range(count):
            uv = unpack(messages[at])[3:5]
            normal = jnp.sqrt(1.0 - uv[0:1] * uv[0:1] - uv[1:2] * uv[1:2])
            pad = jnp.zeros((5, lanes), F32)
            base = which * size + at * lanes
            columns[base : base + lanes, :] = jnp.concatenate([uv, normal, pad], axis=0).T
    for which, points in enumerate((own_points, far_points)):
        for at in range(2):
            base = (2 * which + at) * lanes
            for k, row in enumerate(point_rows(points, at)[:3]):
                rows[k : k + 1, base : base + lanes] = points[row : row + 1, :]
    for which in range(2):
        kernel_re, kernel_im = outs[2 * which : 2 * which + 2]

        def one(at, carry):
            start = pl.multiple_of(at * TILE, TILE)
            here = pl.ds(start, TILE)
            from_ = pl.ds(pl.multiple_of(which * size + start, TILE), TILE)
            turns = (
                columns[from_, 0:1] * rows[0:1, :]
                + columns[from_, 1:2] * rows[1:2, :]
                + columns[from_, 2:3] * rows[2:3, :]
            )
            sine, cosine = half_turns(turns, False)
            kernel_re[here, :] = (1.0 - sine * sine).astype(BF16)
            kernel_im[here, :] = (sine * cosine).astype(BF16)
            return carry

        lax.fori_loop(0, size // TILE, one, 0, unroll=16)


def radiate(kernel_re, kernel_im, held, held_turned):
    return jnp.dot(kernel_re[...], held[...], preferred_element_type=F32) + jnp.dot(
        kernel_im[...], held_turned[...], preferred_element_type=F32
    )


def side_body(mine, theirs, kernel_re, kernel_im, held, held_turned, *outs):
    half, lanes = mine.shape[0] // 2, mine.shape[1]
    is_real = lax.broadcasted_iota(jnp.int32, (half, lanes), 1) < lanes // 2
    for here, there in ((slice(0, half), slice(half, None)), (slice(half, None), slice(0, half))):
        total = mine[here, :] + theirs[there, :].astype(F32)
        moved = pltpu.roll(total, lanes // 2, 1)
        held[here, :] = total.astype(BF16)
        held_turned[here, :] = jnp.where(is_real, -moved, moved).astype(BF16)
    total, start = radiate(kernel_re, kernel_im, held, held_turned), 0
    for out in outs:
        out[...] = total[start : start + out.shape[0]].astype(out.dtype)
        start += out.shape[0]


def near_body(held, held_turned, kernel_re, kernel_im, out):
    out[...] = radiate(kernel_re, kernel_im, held, held_turned)


def fold_body(start, mine, theirs, *outs):
    rows = theirs.shape[0]
    total, at = mine[start : start + rows, :] + theirs[...].astype(F32), 0
    for out in outs:
        out[...] = total[at : at + out.shape[0]].astype(out.dtype)
        at += out.shape[0]


def pass_body(*refs):
    total = refs[0][...].astype(F32)
    for ref in refs[1:-1]:
        total = total + ref[...].astype(F32)
    refs[-1][...] = total.astype(BF16)


def finish_body(kept, *refs):
    total = kept[...]
    rows = total.shape[0]
    for ref in refs[:-1]:
        total = total + ref[0:rows, :].astype(F32)
    refs[-1][...] = total


def call(body, outs, scratch=(), flops=0, anywhere=0, room=32 << 20):
    places = [pl.BlockSpec(memory_space=pltpu.HBM)] * anywhere
    return pl.pallas_call(
        body,
        out_shape=[jax.ShapeDtypeStruct(*out) for out in outs],
        scratch_shapes=list(scratch),
        compiler_params=pltpu.CompilerParams(vmem_limit_bytes=room),
        cost_estimate=pl.CostEstimate(flops=flops, bytes_accessed=0, transcendentals=0),
        **(dict(in_specs=places) if anywhere else {}),
    )


def per_device(
    feed_plane,
    feed_height,
    feed_weights,
    point_plane,
    point_height,
    patch_factor,
    direction_cosines,
):
    size = lax.axis_size("refl")
    line = size // 4
    sources, lanes = feed_weights.shape
    local_points = point_height.shape[0]
    half_points = 2 * local_points
    directions = direction_cosines.shape[1]

    def pairs(step):
        out = []
        for at in range(size):
            row, place = divmod(at, 4)
            far, near = divmod(step, 4)
            to = (row ^ far) if line & (line - 1) == 0 else (row + far) % line
            out.append((at, to * 4 + (place ^ near)))
        return out

    def swap(x, step, back=False, odd_step=None):
        links = pairs(step)
        if odd_step is not None:
            links = links[::2] + pairs(odd_step)[1::2]
        return lax.ppermute(x, "refl", [(b, a) for a, b in links] if back else links)

    message, points = call(
        pack_body,
        [((sources + PACK_ROWS, lanes), BF16), ((8, lanes), F32)],
        [pltpu.VMEM((8, lanes), F32), pltpu.VMEM((2, 2 * lanes), F32), pltpu.SemaphoreType.DMA((7,))],
        anywhere=7,
        room=32 << 20,
    )(
        *[
            pltpu.with_memory_space_constraint(x, pltpu.HBM)
            for x in (
                feed_weights,
                feed_plane,
                feed_height.reshape(1, lanes),
                direction_cosines,
                point_plane,
                point_height.reshape(2, lanes),
                patch_factor.reshape(2, lanes),
            )
        ]
    )
    arrived = [swap(message, 4 * k + 1) for k in range(1, line)]
    far_points = swap(points, 3)
    far_points, *arrived = lax.optimization_barrier((far_points, *arrived))
    near_messages = jnp.stack([message, *arrived])
    side_messages = swap(near_messages, 1)

    part = line * sources
    chunk = local_points
    scale = 1.0 / math.sqrt(local_points * size)

    def green(points, messages, bases, types):
        rows = len(points) * local_points
        slot = [((chunk, part), BF16), ((chunk, part), BF16), ((chunk, part), F32)]
        tables = [] if bases else [((rows, 4), F32), ((rows, TERMS), BF16)]
        scratch = [
            ((8, part), F32),
            ((TERMS, part), BF16),
            ((part, lanes), BF16),
            ((part, lanes), BF16),
            *slot,
            *slot,
        ]
        scratch = [pltpu.VMEM(*which) for which in scratch]
        return call(
            functools.partial(green_body, len(points), len(bases[:1]), scale),
            [((rows, lanes), kind) for kind in types] + tables,
            scratch,
            0,
        )(*points, messages, *bases)

    sets = [points, far_points]
    first, *tables = green(sets, near_messages, [], [F32])
    mine, told = green(sets, side_messages, [first, *tables], [F32, BF16])
    theirs = swap(told, 3)

    even = lax.rem(lax.axis_index("refl"), 2) == 0
    near, side = ([x[k, sources:] for k in range(line)] for x in (near_messages, side_messages))
    keep, give = [near[0]], [side[0]]
    middle = [line // 2] if line % 2 == 0 and line > 1 else []
    for k in middle:
        keep.append(near[k])
        give.append(side[k])
    couples = [(k, line - k) for k in range(1, (line + 1) // 2)]
    for low, high in couples:
        keep += [jnp.where(even, side[low], side[high]), jnp.where(even, near[low], near[high])]
        give += [jnp.where(even, near[high], near[low]), jnp.where(even, side[high], side[low])]

    count = line * directions
    near_re, near_im, side_re, side_im = call(
        kernel_body,
        [((count, half_points), BF16)] * 4,
        [pltpu.VMEM((2 * count, 8), F32), pltpu.VMEM((8, half_points), F32)],
        60 * count * half_points,
    )(points, far_points, jnp.stack(keep), jnp.stack(give))
    block, double = (directions, lanes), (2 * directions, lanes)
    parts = [[(block, F32)] + [(block, BF16)] * len(middle), [(double, BF16)] * len(couples)]
    parts = [part for part in parts if part]
    lengths = [sum(shape[0] for shape, _ in part) for part in parts]
    held, held_turned, *told = call(
        side_body,
        [((half_points, lanes), BF16)] * 2 + [((rows, lanes), BF16) for rows in lengths],
    )(mine, theirs, side_re, side_im)
    given = [swap(x, 1) for x in told[::-1]][::-1]
    near = call(near_body, [((count, lanes), F32)])(held, held_turned, near_re, near_im)[0]
    folded = [
        call(functools.partial(fold_body, sum(lengths[:at])), part)(near, given[at])
        for at, part in enumerate(parts)
    ]
    kept, *sent = [x for group in folded for x in group]
    doubles = [
        swap(x, 4 * low, back=True, odd_step=4 * high)
        for x, (low, high) in zip(sent[len(middle) :], couples)
    ]
    singles = [swap(x, 4 * k + 1, back=True) for x, k in zip(sent, middle)]
    arrived = singles + doubles
    if doubles:
        passed = [x[directions:] for x in doubles]
        if len(passed) > 1:
            passed = call(pass_body, [(block, BF16)])(*passed)
        arrived.append(swap(passed[0], 1))
    return call(finish_body, [((directions, lanes), F32)])(kept, *arrived)[0]


def solution(mesh):
    in_specs = (
        P("grp", "refl"),
        P(("grp", "refl")),
        P("refl", "grp"),
        P("grp", "refl"),
        P(("grp", "refl")),
        P(("grp", "refl")),
        P(None, "refl"),
    )
    out_specs = P("refl", "grp")
    return jax.shard_map(
        per_device, mesh=mesh, in_specs=in_specs, out_specs=out_specs, check_vma=False
    )
```

```python
import functools
import math

import jax
import jax.numpy as jnp
from jax import lax
from jax.experimental import pallas as pl
from jax.experimental.pallas import tpu as pltpu
from jax.sharding import PartitionSpec as P

RANGE_REF = 20.0
F32, BF16 = jnp.float32, jnp.bfloat16

SIN_HALF = (3.1415898893585, -5.167370491466989, 2.5435336188246254, -0.557959530770679)

ROUNDER = 1.5 * 2.0**23

TERMS = 32
MIDDLE = 22.0

COORDS = 5
PACK_ROWS = 16


def horner(square, terms, scale):
    total = jnp.float32(terms[-1] * scale)
    for term in terms[-2::-1]:
        total = total * square + jnp.float32(term * scale)
    return total


def half_turns(turns, flip):
    whole = (turns + ROUNDER) - ROUNDER
    part = whole - turns if flip else turns - whole
    sine = part * horner(part * part, SIN_HALF, math.sqrt(2.0))
    rest = jnp.maximum(2.0 - sine * sine, 1e-12)
    return sine, rest * lax.rsqrt(rest)


def turned(columns):
    half = columns.shape[1] // 2
    return jnp.concatenate([-columns[:, half:], columns[:, :half]], axis=1)


def pack_body(
    weights, feed_plane, feed_height, cosines, plane, height, patch, message, points, coords, ends, sems
):
    rows, lanes = weights.shape
    sources = [feed_plane, feed_height, cosines, plane, height, patch, weights]
    targets = [
        coords.at[0:2, :],
        coords.at[2:3, :],
        coords.at[3:5, :],
        ends,
        points.at[4:6, :],
        points.at[6:8, :],
        message.at[0:rows, :],
    ]
    copies = [
        pltpu.make_async_copy(source, target, sems.at[at])
        for at, (source, target) in enumerate(zip(sources, targets))
    ]
    for copy in copies[::-1]:
        copy.start()
    for copy in copies[:4]:
        copy.wait()
    points[0:2, :] = ends[:, :lanes]
    points[2:4, :] = ends[:, lanes:]
    exact = coords[0:COORDS, :]
    high = exact.astype(BF16)
    rest = exact - high.astype(F32)
    middle = rest.astype(BF16)
    low = (rest - middle.astype(F32)).astype(BF16)
    pad = jnp.zeros((PACK_ROWS - 3 * COORDS, lanes), F32)
    message[rows:, :] = jnp.concatenate(
        [high.astype(F32), middle.astype(F32), low.astype(F32), pad], axis=0
    ).astype(BF16)
    for copy in copies[4:]:
        copy.wait()


def unpack(tail):
    tail = tail.astype(F32)
    return (tail[:COORDS] + tail[COORDS : 2 * COORDS]) + tail[2 * COORDS : 3 * COORDS]


def split(value):
    high = value.astype(BF16).astype(F32)
    rest = value - high
    middle = rest.astype(BF16).astype(F32)
    return high, middle, (rest - middle).astype(BF16).astype(F32)


def distance_terms(x, y, z, is_point):
    z = z - MIDDLE
    square = x * x + y * y + z * z
    out = []
    for value in (x, y, z):
        high, middle, low = split(value if is_point else -2.0 * value)
        out += [high, high, middle, high, middle, low] if is_point else [high, middle, high, low, middle, high]
    ones = [jnp.ones_like(x)] * 3
    out += list(split(square)) + ones if is_point else ones + list(split(square))
    return jnp.concatenate(out + [jnp.zeros_like(x)] * (TERMS - len(out)), axis=0)


def point_rows(points, at):
    return (2 * at, 2 * at + 1, 4 + at, 6 + at)


def fill_point_columns(points, columns, base):
    lanes = points.shape[1]
    up = points[...].T
    for at in range(2):
        columns[base + at * lanes : base + (at + 1) * lanes, :] = jnp.concatenate(
            [up[:, k : k + 1] for k in point_rows(points, at)], axis=1
        )


TILE = 32
LANES = 256


def blocks(total, most):
    return [slice(at, min(at + most, total)) for at in range(0, total, most)]


def green_body(point_sets, bases, scale, *refs):
    points, messages, refs = refs[:point_sets], refs[point_sets], refs[point_sets + 1 :]
    if bases:
        base, (columns, left), outs = refs[:bases], refs[bases : bases + 2], refs[bases + 2 : -10]
    else:
        base, outs, (columns, left) = (), refs[:-12], refs[-12:-10]
    heights, right, weights, weights_turned, *slots = refs[-10:]
    slots = (slots[:3], slots[3:])
    count, height, lanes = messages.shape
    sources = height - PACK_ROWS
    total_points = columns.shape[0]
    for at in range(0 if bases else point_sets):
        fill_point_columns(points[at], columns, 2 * lanes * at)
        for half in range(2):
            x, y, z = (points[at][k : k + 1, :] for k in point_rows(points[at], half)[:3])
            start = (2 * at + half) * lanes
            left[start : start + lanes, :] = distance_terms(x, y, z, True).T.astype(BF16)
    for at in range(count):
        where = slice(at * sources, (at + 1) * sources)
        coords = unpack(messages[at, sources:, :])
        x, y, z = coords[0:1], coords[1:2], coords[2:3]
        heights[0:1, where] = z * RANGE_REF
        right[:, where] = distance_terms(x, y, z, False).astype(BF16)
        block = messages[at, :sources, :]
        weights[where, :] = block
        weights_turned[where, :] = turned(block)
    chunk = slots[0][0].shape[0]

    def fill(start, green_re, green_im, squares):
        squares[...] = jnp.dot(
            left[start : start + chunk, :], right[...], preferred_element_type=F32
        )
        for at in range(0, chunk, TILE):
            low = columns[start + at : start + at + TILE, 2:3] * RANGE_REF
            for part in blocks(count * sources, LANES):
                squared = squares[at : at + TILE, part]
                inverse = lax.rsqrt(squared)
                sine, cosine = half_turns(squared * inverse, True)
                amplitude = (heights[0:1, part] - low) * (inverse * inverse)
                scaled = amplitude * sine
                green_re[at : at + TILE, part] = (amplitude - scaled * sine).astype(BF16)
                green_im[at : at + TILE, part] = (scaled * cosine).astype(BF16)

    def add_up(start, green_re, green_im, _):
        here = slice(start, start + chunk)
        total = jnp.dot(green_re[...], weights[...], preferred_element_type=F32) + jnp.dot(
            green_im[...], weights_turned[...], preferred_element_type=F32
        )
        if base:
            step = base[0].shape[0]
            held = base[start // step][start % step : start % step + chunk, :]
            total = (total + held) * (columns[here, 3:4] * scale)
        for out in outs:
            out[here, :] = total.astype(out.dtype)

    turns = total_points // chunk
    for at in range(turns + 1):
        if at < turns:
            fill(at * chunk, *slots[at % 2])
        if at > 0:
            add_up((at - 1) * chunk, *slots[(at - 1) % 2])


def kernel_body(own_points, far_points, *refs):
    groups = refs[:2]
    outs = refs[2:6]
    columns, rows = refs[6:]
    count, _, lanes = groups[0].shape
    size = count * lanes
    for which, messages in enumerate(groups):
        for at in range(count):
            uv = unpack(messages[at])[3:5]
            normal = jnp.sqrt(1.0 - uv[0:1] * uv[0:1] - uv[1:2] * uv[1:2])
            pad = jnp.zeros((5, lanes), F32)
            base = which * size + at * lanes
            columns[base : base + lanes, :] = jnp.concatenate([uv, normal, pad], axis=0).T
    for which, points in enumerate((own_points, far_points)):
        for at in range(2):
            base = (2 * which + at) * lanes
            for k, row in enumerate(point_rows(points, at)[:3]):
                rows[k : k + 1, base : base + lanes] = points[row : row + 1, :]
    for which in range(2):
        kernel_re, kernel_im = outs[2 * which : 2 * which + 2]

        def one(at, carry):
            start = pl.multiple_of(at * TILE, TILE)
            here = pl.ds(start, TILE)
            from_ = pl.ds(pl.multiple_of(which * size + start, TILE), TILE)
            turns = (
                columns[from_, 0:1] * rows[0:1, :]
                + columns[from_, 1:2] * rows[1:2, :]
                + columns[from_, 2:3] * rows[2:3, :]
            )
            sine, cosine = half_turns(turns, False)
            kernel_re[here, :] = (1.0 - sine * sine).astype(BF16)
            kernel_im[here, :] = (sine * cosine).astype(BF16)
            return carry

        lax.fori_loop(0, size // TILE, one, 0, unroll=16)


def radiate(kernel_re, kernel_im, held, held_turned):
    return jnp.dot(kernel_re[...], held[...], preferred_element_type=F32) + jnp.dot(
        kernel_im[...], held_turned[...], preferred_element_type=F32
    )


def side_body(mine, theirs, kernel_re, kernel_im, held, held_turned, *outs):
    half, lanes = mine.shape[0] // 2, mine.shape[1]
    is_real = lax.broadcasted_iota(jnp.int32, (half, lanes), 1) < lanes // 2
    for here, there in ((slice(0, half), slice(half, None)), (slice(half, None), slice(0, half))):
        total = mine[here, :] + theirs[there, :].astype(F32)
        moved = pltpu.roll(total, lanes // 2, 1)
        held[here, :] = total.astype(BF16)
        held_turned[here, :] = jnp.where(is_real, -moved, moved).astype(BF16)
    total, start = radiate(kernel_re, kernel_im, held, held_turned), 0
    for out in outs:
        out[...] = total[start : start + out.shape[0]].astype(out.dtype)
        start += out.shape[0]


def near_body(held, held_turned, kernel_re, kernel_im, out):
    out[...] = radiate(kernel_re, kernel_im, held, held_turned)


def fold_body(start, mine, theirs, *outs):
    rows = theirs.shape[0]
    total, at = mine[start : start + rows, :] + theirs[...].astype(F32), 0
    for out in outs:
        out[...] = total[at : at + out.shape[0]].astype(out.dtype)
        at += out.shape[0]


def pass_body(*refs):
    total = refs[0][...].astype(F32)
    for ref in refs[1:-1]:
        total = total + ref[...].astype(F32)
    refs[-1][...] = total.astype(BF16)


def finish_body(kept, *refs):
    total = kept[...]
    rows = total.shape[0]
    for ref in refs[:-1]:
        total = total + ref[0:rows, :].astype(F32)
    refs[-1][...] = total


def call(body, outs, scratch=(), flops=0, anywhere=0, room=32 << 20):
    places = [pl.BlockSpec(memory_space=pltpu.HBM)] * anywhere
    return pl.pallas_call(
        body,
        out_shape=[jax.ShapeDtypeStruct(*out) for out in outs],
        scratch_shapes=list(scratch),
        compiler_params=pltpu.CompilerParams(vmem_limit_bytes=room),
        cost_estimate=pl.CostEstimate(flops=flops, bytes_accessed=0, transcendentals=0),
        **(dict(in_specs=places) if anywhere else {}),
    )


def per_device(
    feed_plane,
    feed_height,
    feed_weights,
    point_plane,
    point_height,
    patch_factor,
    direction_cosines,
):
    size = lax.axis_size("refl")
    line = size // 4
    sources, lanes = feed_weights.shape
    local_points = point_height.shape[0]
    half_points = 2 * local_points
    directions = direction_cosines.shape[1]

    def pairs(step):
        out = []
        for at in range(size):
            row, place = divmod(at, 4)
            far, near = divmod(step, 4)
            to = (row ^ far) if line & (line - 1) == 0 else (row + far) % line
            out.append((at, to * 4 + (place ^ near)))
        return out

    def swap(x, step, back=False, odd_step=None):
        links = pairs(step)
        if odd_step is not None:
            links = links[::2] + pairs(odd_step)[1::2]
        return lax.ppermute(x, "refl", [(b, a) for a, b in links] if back else links)

    message, points = call(
        pack_body,
        [((sources + PACK_ROWS, lanes), BF16), ((8, lanes), F32)],
        [pltpu.VMEM((8, lanes), F32), pltpu.VMEM((2, 2 * lanes), F32), pltpu.SemaphoreType.DMA((7,))],
        anywhere=7,
        room=32 << 20,
    )(
        *[
            pltpu.with_memory_space_constraint(x, pltpu.HBM)
            for x in (
                feed_weights,
                feed_plane,
                feed_height.reshape(1, lanes),
                direction_cosines,
                point_plane,
                point_height.reshape(2, lanes),
                patch_factor.reshape(2, lanes),
            )
        ]
    )
    arrived = [swap(message, 4 * k + 1) for k in range(1, line)]
    far_points = swap(points, 3)
    far_points, *arrived = lax.optimization_barrier((far_points, *arrived))
    near_messages = jnp.stack([message, *arrived])
    side_messages = swap(near_messages, 1)

    part = line * sources
    chunk = local_points
    scale = 1.0 / math.sqrt(local_points * size)

    def green(points, messages, bases, types):
        rows = len(points) * local_points
        slot = [((chunk, part), BF16), ((chunk, part), BF16), ((chunk, part), F32)]
        tables = [] if bases else [((rows, 4), F32), ((rows, TERMS), BF16)]
        scratch = [
            ((8, part), F32),
            ((TERMS, part), BF16),
            ((part, lanes), BF16),
            ((part, lanes), BF16),
            *slot,
            *slot,
        ]
        scratch = [pltpu.VMEM(*which) for which in scratch]
        return call(
            functools.partial(green_body, len(points), len(bases[:1]), scale),
            [((rows, lanes), kind) for kind in types] + tables,
            scratch,
            0,
        )(*points, messages, *bases)

    sets = [points, far_points]
    first, *tables = green(sets, near_messages, [], [F32])
    mine, told = green(sets, side_messages, [first, *tables], [F32, BF16])
    theirs = swap(told, 3)

    even = lax.rem(lax.axis_index("refl"), 2) == 0
    near, side = ([x[k, sources:] for k in range(line)] for x in (near_messages, side_messages))
    keep, give = [near[0]], [side[0]]
    middle = [line // 2] if line % 2 == 0 and line > 1 else []
    for k in middle:
        keep.append(near[k])
        give.append(side[k])
    couples = [(k, line - k) for k in range(1, (line + 1) // 2)]
    for low, high in couples:
        keep += [jnp.where(even, side[low], side[high]), jnp.where(even, near[low], near[high])]
        give += [jnp.where(even, near[high], near[low]), jnp.where(even, side[high], side[low])]

    count = line * directions
    near_re, near_im, side_re, side_im = call(
        kernel_body,
        [((count, half_points), BF16)] * 4,
        [pltpu.VMEM((2 * count, 8), F32), pltpu.VMEM((8, half_points), F32)],
        60 * count * half_points,
    )(points, far_points, jnp.stack(keep), jnp.stack(give))
    block, double = (directions, lanes), (2 * directions, lanes)
    parts = [[(block, F32)] + [(block, BF16)] * len(middle), [(double, BF16)] * len(couples)]
    parts = [part for part in parts if part]
    lengths = [sum(shape[0] for shape, _ in part) for part in parts]
    held, held_turned, *told = call(
        side_body,
        [((half_points, lanes), BF16)] * 2 + [((rows, lanes), BF16) for rows in lengths],
    )(mine, theirs, side_re, side_im)
    given = [swap(x, 1) for x in told[::-1]][::-1]
    near = call(near_body, [((count, lanes), F32)])(held, held_turned, near_re, near_im)[0]
    folded = [
        call(functools.partial(fold_body, sum(lengths[:at])), part)(near, given[at])
        for at, part in enumerate(parts)
    ]
    kept, *sent = [x for group in folded for x in group]
    doubles = [
        swap(x, 4 * low, back=True, odd_step=4 * high)
        for x, (low, high) in zip(sent[len(middle) :], couples)
    ]
    singles = [swap(x, 4 * k + 1, back=True) for x, k in zip(sent, middle)]
    arrived = singles + doubles
    if doubles:
        passed = [x[directions:] for x in doubles]
        if len(passed) > 1:
            passed = call(pass_body, [(block, BF16)])(*passed)
        arrived.append(swap(passed[0], 1))
    return call(finish_body, [((directions, lanes), F32)])(kept, *arrived)[0]


def solution(mesh):
    in_specs = (
        P("grp", "refl"),
        P(("grp", "refl")),
        P("refl", "grp"),
        P("grp", "refl"),
        P(("grp", "refl")),
        P(("grp", "refl")),
        P(None, "refl"),
    )
    out_specs = P("refl", "grp")
    return jax.shard_map(
        per_device, mesh=mesh, in_specs=in_specs, out_specs=out_specs, check_vma=False
    )
```

```python
import functools
import math

import jax
import jax.numpy as jnp
from jax import lax
from jax.experimental import pallas as pl
from jax.experimental.pallas import tpu as pltpu
from jax.sharding import PartitionSpec as P

RANGE_REF = 20.0
F32, BF16 = jnp.float32, jnp.bfloat16

SIN_HALF = (3.1415898893585, -5.167370491466989, 2.5435336188246254, -0.557959530770679)

ROUNDER = 1.5 * 2.0**23

TERMS = 32
MIDDLE = 22.0

COORDS = 5
PACK_ROWS = 16


def horner(square, terms, scale):
    total = jnp.float32(terms[-1] * scale)
    for term in terms[-2::-1]:
        total = total * square + jnp.float32(term * scale)
    return total


def half_turns(turns, flip):
    whole = (turns + ROUNDER) - ROUNDER
    part = whole - turns if flip else turns - whole
    sine = part * horner(part * part, SIN_HALF, math.sqrt(2.0))
    rest = jnp.maximum(2.0 - sine * sine, 1e-12)
    return sine, rest * lax.rsqrt(rest)


def turned(columns):
    half = columns.shape[1] // 2
    return jnp.concatenate([-columns[:, half:], columns[:, :half]], axis=1)


def pack_body(
    weights, feed_plane, feed_height, cosines, plane, height, patch, message, points, coords, ends, sems
):
    rows, lanes = weights.shape
    sources = [feed_plane, feed_height, cosines, plane, height, patch, weights]
    targets = [
        coords.at[0:2, :],
        coords.at[2:3, :],
        coords.at[3:5, :],
        ends,
        points.at[4:6, :],
        points.at[6:8, :],
        message.at[0:rows, :],
    ]
    copies = [
        pltpu.make_async_copy(source, target, sems.at[at])
        for at, (source, target) in enumerate(zip(sources, targets))
    ]
    for copy in copies[::-1]:
        copy.start()
    for copy in copies[:4]:
        copy.wait()
    points[0:2, :] = ends[:, :lanes]
    points[2:4, :] = ends[:, lanes:]
    exact = coords[0:COORDS, :]
    high = exact.astype(BF16)
    rest = exact - high.astype(F32)
    middle = rest.astype(BF16)
    low = (rest - middle.astype(F32)).astype(BF16)
    pad = jnp.zeros((PACK_ROWS - 3 * COORDS, lanes), F32)
    message[rows:, :] = jnp.concatenate(
        [high.astype(F32), middle.astype(F32), low.astype(F32), pad], axis=0
    ).astype(BF16)
    for copy in copies[4:]:
        copy.wait()


def unpack(tail):
    tail = tail.astype(F32)
    return (tail[:COORDS] + tail[COORDS : 2 * COORDS]) + tail[2 * COORDS : 3 * COORDS]


def split(value):
    high = value.astype(BF16).astype(F32)
    rest = value - high
    middle = rest.astype(BF16).astype(F32)
    return high, middle, (rest - middle).astype(BF16).astype(F32)


def distance_terms(x, y, z, is_point):
    z = z - MIDDLE
    square = x * x + y * y + z * z
    out = []
    for value in (x, y, z):
        high, middle, low = split(value if is_point else -2.0 * value)
        out += [high, high, middle, high, middle, low] if is_point else [high, middle, high, low, middle, high]
    ones = [jnp.ones_like(x)] * 3
    out += list(split(square)) + ones if is_point else ones + list(split(square))
    return jnp.concatenate(out + [jnp.zeros_like(x)] * (TERMS - len(out)), axis=0)


def point_rows(points, at):
    return (2 * at, 2 * at + 1, 4 + at, 6 + at)


def fill_point_columns(points, columns, base):
    lanes = points.shape[1]
    up = points[...].T
    for at in range(2):
        columns[base + at * lanes : base + (at + 1) * lanes, :] = jnp.concatenate(
            [up[:, k : k + 1] for k in point_rows(points, at)], axis=1
        )


TILE = 32
LANES = 128


def blocks(total, most):
    return [slice(at, min(at + most, total)) for at in range(0, total, most)]


def green_body(point_sets, bases, scale, *refs):
    points, messages, refs = refs[:point_sets], refs[point_sets], refs[point_sets + 1 :]
    if bases:
        base, (columns, left), outs = refs[:bases], refs[bases : bases + 2], refs[bases + 2 : -10]
    else:
        base, outs, (columns, left) = (), refs[:-12], refs[-12:-10]
    heights, right, weights, weights_turned, *slots = refs[-10:]
    slots = (slots[:3], slots[3:])
    count, height, lanes = messages.shape
    sources = height - PACK_ROWS
    total_points = columns.shape[0]
    for at in range(0 if bases else point_sets):
        fill_point_columns(points[at], columns, 2 * lanes * at)
        for half in range(2):
            x, y, z = (points[at][k : k + 1, :] for k in point_rows(points[at], half)[:3])
            start = (2 * at + half) * lanes
            left[start : start + lanes, :] = distance_terms(x, y, z, True).T.astype(BF16)
    for at in range(count):
        where = slice(at * sources, (at + 1) * sources)
        coords = unpack(messages[at, sources:, :])
        x, y, z = coords[0:1], coords[1:2], coords[2:3]
        heights[0:1, where] = z * RANGE_REF
        right[:, where] = distance_terms(x, y, z, False).astype(BF16)
        block = messages[at, :sources, :]
        weights[where, :] = block
        weights_turned[where, :] = turned(block)
    chunk = slots[0][0].shape[0]

    def fill(start, green_re, green_im, squares):
        squares[...] = jnp.dot(
            left[start : start + chunk, :], right[...], preferred_element_type=F32
        )
        for at in range(0, chunk, TILE):
            low = columns[start + at : start + at + TILE, 2:3] * RANGE_REF
            for part in blocks(count * sources, LANES):
                squared = squares[at : at + TILE, part]
                inverse = lax.rsqrt(squared)
                sine, cosine = half_turns(squared * inverse, True)
                amplitude = (heights[0:1, part] - low) * (inverse * inverse)
                scaled = amplitude * sine
                green_re[at : at + TILE, part] = (amplitude - scaled * sine).astype(BF16)
                green_im[at : at + TILE, part] = (scaled * cosine).astype(BF16)

    def add_up(start, green_re, green_im, _):
        here = slice(start, start + chunk)
        total = jnp.dot(green_re[...], weights[...], preferred_element_type=F32) + jnp.dot(
            green_im[...], weights_turned[...], preferred_element_type=F32
        )
        if base:
            step = base[0].shape[0]
            held = base[start // step][start % step : start % step + chunk, :]
            total = (total + held) * (columns[here, 3:4] * scale)
        for out in outs:
            out[here, :] = total.astype(out.dtype)

    turns = total_points // chunk
    for at in range(turns + 1):
        if at < turns:
            fill(at * chunk, *slots[at % 2])
        if at > 0:
            add_up((at - 1) * chunk, *slots[(at - 1) % 2])


def kernel_body(own_points, far_points, *refs):
    groups = refs[:2]
    outs = refs[2:6]
    columns, rows = refs[6:]
    count, _, lanes = groups[0].shape
    size = count * lanes
    for which, messages in enumerate(groups):
        for at in range(count):
            uv = unpack(messages[at])[3:5]
            normal = jnp.sqrt(1.0 - uv[0:1] * uv[0:1] - uv[1:2] * uv[1:2])
            pad = jnp.zeros((5, lanes), F32)
            base = which * size + at * lanes
            columns[base : base + lanes, :] = jnp.concatenate([uv, normal, pad], axis=0).T
    for which, points in enumerate((own_points, far_points)):
        for at in range(2):
            base = (2 * which + at) * lanes
            for k, row in enumerate(point_rows(points, at)[:3]):
                rows[k : k + 1, base : base + lanes] = points[row : row + 1, :]
    for which in range(2):
        kernel_re, kernel_im = outs[2 * which : 2 * which + 2]

        def one(at, carry):
            start = pl.multiple_of(at * TILE, TILE)
            here = pl.ds(start, TILE)
            from_ = pl.ds(pl.multiple_of(which * size + start, TILE), TILE)
            turns = (
                columns[from_, 0:1] * rows[0:1, :]
                + columns[from_, 1:2] * rows[1:2, :]
                + columns[from_, 2:3] * rows[2:3, :]
            )
            sine, cosine = half_turns(turns, False)
            kernel_re[here, :] = (1.0 - sine * sine).astype(BF16)
            kernel_im[here, :] = (sine * cosine).astype(BF16)
            return carry

        lax.fori_loop(0, size // TILE, one, 0, unroll=16)


def radiate(kernel_re, kernel_im, held, held_turned):
    return jnp.dot(kernel_re[...], held[...], preferred_element_type=F32) + jnp.dot(
        kernel_im[...], held_turned[...], preferred_element_type=F32
    )


def side_body(mine, theirs, kernel_re, kernel_im, held, held_turned, *outs):
    half, lanes = mine.shape[0] // 2, mine.shape[1]
    is_real = lax.broadcasted_iota(jnp.int32, (half, lanes), 1) < lanes // 2
    for here, there in ((slice(0, half), slice(half, None)), (slice(half, None), slice(0, half))):
        total = mine[here, :] + theirs[there, :].astype(F32)
        moved = pltpu.roll(total, lanes // 2, 1)
        held[here, :] = total.astype(BF16)
        held_turned[here, :] = jnp.where(is_real, -moved, moved).astype(BF16)
    total, start = radiate(kernel_re, kernel_im, held, held_turned), 0
    for out in outs:
        out[...] = total[start : start + out.shape[0]].astype(out.dtype)
        start += out.shape[0]


def near_body(held, held_turned, kernel_re, kernel_im, out):
    out[...] = radiate(kernel_re, kernel_im, held, held_turned)


def fold_body(start, mine, theirs, *outs):
    rows = theirs.shape[0]
    total, at = mine[start : start + rows, :] + theirs[...].astype(F32), 0
    for out in outs:
        out[...] = total[at : at + out.shape[0]].astype(out.dtype)
        at += out.shape[0]


def pass_body(*refs):
    total = refs[0][...].astype(F32)
    for ref in refs[1:-1]:
        total = total + ref[...].astype(F32)
    refs[-1][...] = total.astype(BF16)


def finish_body(kept, *refs):
    total = kept[...]
    rows = total.shape[0]
    for ref in refs[:-1]:
        total = total + ref[0:rows, :].astype(F32)
    refs[-1][...] = total


def call(body, outs, scratch=(), flops=0, anywhere=0, room=32 << 20):
    places = [pl.BlockSpec(memory_space=pltpu.HBM)] * anywhere
    return pl.pallas_call(
        body,
        out_shape=[jax.ShapeDtypeStruct(*out) for out in outs],
        scratch_shapes=list(scratch),
        compiler_params=pltpu.CompilerParams(vmem_limit_bytes=room),
        cost_estimate=pl.CostEstimate(flops=flops, bytes_accessed=0, transcendentals=0),
        **(dict(in_specs=places) if anywhere else {}),
    )


def per_device(
    feed_plane,
    feed_height,
    feed_weights,
    point_plane,
    point_height,
    patch_factor,
    direction_cosines,
):
    size = lax.axis_size("refl")
    line = size // 4
    sources, lanes = feed_weights.shape
    local_points = point_height.shape[0]
    half_points = 2 * local_points
    directions = direction_cosines.shape[1]

    def pairs(step):
        out = []
        for at in range(size):
            row, place = divmod(at, 4)
            far, near = divmod(step, 4)
            to = (row ^ far) if line & (line - 1) == 0 else (row + far) % line
            out.append((at, to * 4 + (place ^ near)))
        return out

    def swap(x, step, back=False, odd_step=None):
        links = pairs(step)
        if odd_step is not None:
            links = links[::2] + pairs(odd_step)[1::2]
        return lax.ppermute(x, "refl", [(b, a) for a, b in links] if back else links)

    message, points = call(
        pack_body,
        [((sources + PACK_ROWS, lanes), BF16), ((8, lanes), F32)],
        [pltpu.VMEM((8, lanes), F32), pltpu.VMEM((2, 2 * lanes), F32), pltpu.SemaphoreType.DMA((7,))],
        anywhere=7,
        room=32 << 20,
    )(
        *[
            pltpu.with_memory_space_constraint(x, pltpu.HBM)
            for x in (
                feed_weights,
                feed_plane,
                feed_height.reshape(1, lanes),
                direction_cosines,
                point_plane,
                point_height.reshape(2, lanes),
                patch_factor.reshape(2, lanes),
            )
        ]
    )
    arrived = [swap(message, 4 * k + 1) for k in range(1, line)]
    far_points = swap(points, 3)
    far_points, *arrived = lax.optimization_barrier((far_points, *arrived))
    near_messages = jnp.stack([message, *arrived])
    side_messages = swap(near_messages, 1)

    part = line * sources
    chunk = local_points
    scale = 1.0 / math.sqrt(local_points * size)

    def green(points, messages, bases, types):
        rows = len(points) * local_points
        slot = [((chunk, part), BF16), ((chunk, part), BF16), ((chunk, part), F32)]
        tables = [] if bases else [((rows, 4), F32), ((rows, TERMS), BF16)]
        scratch = [
            ((8, part), F32),
            ((TERMS, part), BF16),
            ((part, lanes), BF16),
            ((part, lanes), BF16),
            *slot,
            *slot,
        ]
        scratch = [pltpu.VMEM(*which) for which in scratch]
        return call(
            functools.partial(green_body, len(points), len(bases[:1]), scale),
            [((rows, lanes), kind) for kind in types] + tables,
            scratch,
            0,
        )(*points, messages, *bases)

    sets = [points, far_points]
    first, *tables = green(sets, near_messages, [], [F32])
    mine, told = green(sets, side_messages, [first, *tables], [F32, BF16])
    theirs = swap(told, 3)

    even = lax.rem(lax.axis_index("refl"), 2) == 0
    near, side = ([x[k, sources:] for k in range(line)] for x in (near_messages, side_messages))
    keep, give = [near[0]], [side[0]]
    middle = [line // 2] if line % 2 == 0 and line > 1 else []
    for k in middle:
        keep.append(near[k])
        give.append(side[k])
    couples = [(k, line - k) for k in range(1, (line + 1) // 2)]
    for low, high in couples:
        keep += [jnp.where(even, side[low], side[high]), jnp.where(even, near[low], near[high])]
        give += [jnp.where(even, near[high], near[low]), jnp.where(even, side[high], side[low])]

    count = line * directions
    near_re, near_im, side_re, side_im = call(
        kernel_body,
        [((count, half_points), BF16)] * 4,
        [pltpu.VMEM((2 * count, 8), F32), pltpu.VMEM((8, half_points), F32)],
        60 * count * half_points,
    )(points, far_points, jnp.stack(keep), jnp.stack(give))
    block, double = (directions, lanes), (2 * directions, lanes)
    parts = [[(block, F32)] + [(block, BF16)] * len(middle), [(double, BF16)] * len(couples)]
    parts = [part for part in parts if part]
    lengths = [sum(shape[0] for shape, _ in part) for part in parts]
    held, held_turned, *told = call(
        side_body,
        [((half_points, lanes), BF16)] * 2 + [((rows, lanes), BF16) for rows in lengths],
    )(mine, theirs, side_re, side_im)
    given = [swap(x, 1) for x in told[::-1]][::-1]
    near = call(near_body, [((count, lanes), F32)])(held, held_turned, near_re, near_im)[0]
    folded = [
        call(functools.partial(fold_body, sum(lengths[:at])), part)(near, given[at])
        for at, part in enumerate(parts)
    ]
    kept, *sent = [x for group in folded for x in group]
    doubles = [
        swap(x, 4 * low, back=True, odd_step=4 * high)
        for x, (low, high) in zip(sent[len(middle) :], couples)
    ]
    singles = [swap(x, 4 * k + 1, back=True) for x, k in zip(sent, middle)]
    arrived = singles + doubles
    if doubles:
        passed = [x[directions:] for x in doubles]
        if len(passed) > 1:
            passed = call(pass_body, [(block, BF16)])(*passed)
        arrived.append(swap(passed[0], 1))
    return call(finish_body, [((directions, lanes), F32)])(kept, *arrived)[0]


def solution(mesh):
    in_specs = (
        P("grp", "refl"),
        P(("grp", "refl")),
        P("refl", "grp"),
        P("grp", "refl"),
        P(("grp", "refl")),
        P(("grp", "refl")),
        P(None, "refl"),
    )
    out_specs = P("refl", "grp")
    return jax.shard_map(
        per_device, mesh=mesh, in_specs=in_specs, out_specs=out_specs, check_vma=False
    )
```
